256 devices in a mesh: seq: 32 (over x, z), head: 8 (over y, core).
Axes of the slice: x: 4, y: 4, z: 8, core: 2. Of those that a mesh axis runs over, the one named last changes fastest.
Arguments:
- queries: bfloat16 [8192, 64, 128], P('seq', 'head')
- keys: bfloat16 [8192, 8, 128], P('seq', 'head')
- block_order: int32 [128], P('seq'), may hold values from 0 to 127, each once
- gate_query: bfloat16 [8, 128, 128], P('head'), may hold values from -0.5 to 0.5
- gate_key: bfloat16 [8, 384, 128], P('head'), may hold values from -0.3125 to 0.3125
Outputs:
- loss: float32 [], replicated
- grad_query: float32 [8, 128, 128], P('head')
- grad_key: float32 [8, 384, 128], P('head')
The draws below stay inside these ranges and needn't reach their ends.
Inputs may be any that keep to these rules, and one draw needn't show every extreme that they name: `block_order`: each block position appears exactly once.
All inputs are finite; a program needn't handle non-finite values.
Results may differ from the reference program's by a relative error of at most 0.0029.
Values may be sent and summed in bfloat16 or wider, within the bound.
No kernel may reach another device: no remote copies, remote signals or barrier semaphores. Data moves between devices by JAX's collectives and lax.ppermute only.
A program may use at most 64 MiB of HBM per device.

```python
import jax
import jax.numpy as jnp
from jax import lax

HD = 128
GROUP = 8
BLOCK = 64
DG = 128
KVH = 8
QH = 64
S = 8192
NB = 128


def shared_keys(key):
    return jnp.clip(jax.random.normal(key, (S, KVH, HD), jnp.float32), -6.0, 6.0)


def draw_keys(key, part):
    return shared_keys(key).astype(jnp.bfloat16)


def draw_queries(key, part):
    key = jax.random.fold_in(key, 7)
    drawn = jnp.clip(jax.random.normal(key, (S, QH, HD), jnp.float32), -6.0, 6.0)
    return drawn.astype(jnp.bfloat16)


def levels(stream_key, dims, shards, low, largest):
    def one(axis_at, blocks):
        draws = jax.random.uniform(jax.random.fold_in(jax.random.fold_in(stream_key, 6), axis_at), (blocks,), jnp.float32, low / len(shards), largest / len(shards))
        return jnp.repeat(jnp.exp(draws), dims[axis_at] // blocks).reshape((-1,) + (1,) * (len(dims) - axis_at - 1))

    factor_of = one(*shards[0])
    for cut in shards[1:]:
        factor_of = factor_of * one(*cut)
    return factor_of


def scatter_about(key, shape, spread, most, shards=(), held_as=jnp.bfloat16):
    factor_of = levels(key, shape, shards, -0.22, 0.18) if shards else 1.0
    array = jax.random.normal(key, shape, jnp.float32) * spread * factor_of
    return jnp.minimum(jnp.maximum(array, -most), most).astype(held_as)


def setup_inputs(seed: int = 0) -> dict:
    splits = jax.random.split(jax.random.key(seed), 6)
    return {
        "queries": draw_queries(jax.random.fold_in(splits[5], 71), 0),
        "keys": draw_keys(jax.random.fold_in(splits[5], 71), 0),
        "block_order": jax.random.permutation(splits[2], NB).astype(jnp.int32),
        "gate_query": scatter_about(splits[3], (KVH, HD, DG), HD ** -0.5, 0.5, ((0, 8),)),
        "gate_key": scatter_about(splits[4], (KVH, 3 * HD, DG), (3 * HD) ** -0.5, 0.3125, ((0, 8),)),
    }


HIGH = lax.Precision.HIGHEST

def pooled_targets(queries, keys, block_order):
    span = 512
    nch = S // span
    offs = jnp.arange(BLOCK, dtype=jnp.int32)
    pos = (block_order[:, None] * BLOCK + offs[None, :]).reshape(S)
    scale = HD ** (-0.5)

    def one(index):
        kvh = index // nch
        part = index % nch
        qs = lax.dynamic_slice(queries, (part * span, kvh * GROUP, jnp.int32(0)), (span, GROUP, HD))
        ks = lax.dynamic_index_in_dim(keys, kvh, 1, keepdims=False)
        qpos = lax.dynamic_slice_in_dim(pos, part * span, span, 0)
        scores = jnp.einsum('tgd,ud->gtu', qs.astype(jnp.float32), ks.astype(jnp.float32)) * scale
        scores = jnp.where(pos[None, None, :] > qpos[None, :, None], -1e+30, scores)
        rmax = lax.optimization_barrier(jnp.max(scores, axis=-1))
        lse = rmax + jnp.log(lax.optimization_barrier(jnp.sum(jnp.exp(scores - rmax[..., None]), axis=-1)))
        bmax = lax.optimization_barrier(jnp.max(scores.reshape(GROUP, span, NB, BLOCK), axis=-1))
        probs = jnp.exp(bmax - lse[..., None])
        return lax.optimization_barrier(jnp.max(probs.reshape(GROUP, span // BLOCK, BLOCK, NB), axis=2))
    out = lax.map(one, jnp.arange(KVH * nch, dtype=jnp.int32))
    out = out.reshape(KVH, nch, GROUP, span // BLOCK, NB).transpose(0, 2, 1, 3, 4).reshape(QH, NB, NB)
    return out / lax.optimization_barrier(jnp.sum(out, axis=-1, keepdims=True))

def reference(queries, keys, block_order, gate_query, gate_key):
    target = pooled_targets(queries, keys, block_order)
    qpool = lax.optimization_barrier(jnp.mean(queries.reshape(NB, BLOCK, QH, HD).astype(jnp.float32), axis=1)).astype(jnp.bfloat16)
    kb = keys.reshape(NB, BLOCK, KVH, HD)
    kmean = lax.optimization_barrier(jnp.mean(kb.astype(jnp.float32), axis=1)).astype(jnp.bfloat16)
    kpool = jnp.concatenate([lax.optimization_barrier(jnp.max(kb, axis=1)), lax.optimization_barrier(jnp.min(kb, axis=1)), kmean], axis=-1)
    mask = block_order[None, :] > block_order[:, None]
    safe = jnp.log(jnp.where(target > 0, target, 1.0))

    def loss_of(wq, wk):
        qproj = jnp.einsum('bkgd,kde->kgbe', qpool.reshape(NB, KVH, GROUP, HD).astype(jnp.float32), wq, precision=HIGH)
        kproj = jnp.einsum('ckd,kde->kce', kpool.astype(jnp.float32), wk, precision=HIGH)
        logits = jnp.einsum('kgbe,kce->kgbc', qproj, kproj, precision=HIGH) * DG ** (-0.5)
        logits = jnp.where(mask[None, None], -1e+30, logits).reshape(QH, NB, NB)
        logp = jax.nn.log_softmax(logits, axis=-1)
        terms = jnp.where(target > 0, target * (safe - logp), 0.0)
        return jnp.sum(terms) / (QH * NB)
    loss, back = jax.vjp(loss_of, gate_query.astype(jnp.float32), gate_key.astype(jnp.float32))
    grad_query, grad_key = back(jnp.float32(1.0))
    return (loss, grad_query, grad_key)
```

```python
import functools
import math

import jax
import jax.numpy as jnp
from jax import lax
from jax.experimental import pallas as pl
from jax.experimental.pallas import tpu as pltpu
from jax.sharding import Mesh, PartitionSpec as P

BLOCK = 64
WIDTH = 128
GROUP = 8
LOCAL = 4
SEQ = 32
NB = LOCAL * SEQ
ROWS = LOCAL * BLOCK
SENT = ROWS + 16
SPAN = 8
LANES = BLOCK * GROUP
SCALE = WIDTH ** -0.5
EXP2 = SCALE * math.log2(math.e)
MASKED = -1e30 * WIDTH ** 0.5
HIGH = lax.Precision.HIGHEST
NT = (((1,), (1,)), ((), ()))
NN = (((1,), (0,)), ((), ()))
F32 = jnp.float32
BF16 = jnp.bfloat16


def dot(a, b, dims=NN, precision=None):
    return lax.dot_general(a, b, dims, precision=precision, preferred_element_type=F32)


def prepare(keys_ref, pos_ref, out_ref):
    keys = keys_ref[...]
    blocks = keys.astype(F32).reshape(LOCAL, BLOCK, WIDTH)
    kmax = jnp.max(blocks, axis=1)
    kmin = jnp.min(blocks, axis=1)
    kmean = jnp.sum(blocks, axis=1) * (1.0 / BLOCK)
    extra = jnp.concatenate([kmax, kmin, kmean, pos_ref[...]], axis=0).astype(BF16)
    for i in range(out_ref.shape[0]):
        out_ref[i, :ROWS, :] = keys
        out_ref[i, ROWS:, :] = extra


def attend(
    pos_sm, own_sm, place_ref, ownrow_ref, gathered_ref, q_ref, wq_ref, wk_ref,
    out_ref, kpool_ref, ks, bm, tgt,
):
    def put(c, _):
        block = gathered_ref[c // LOCAL, pl.ds(pl.multiple_of((c % LOCAL) * BLOCK, BLOCK), BLOCK), :]
        ks[pl.ds(pl.multiple_of(pos_sm[c] * BLOCK, BLOCK), BLOCK), :] = block
        return 0

    lax.fori_loop(0, NB, put, 0, unroll=8)

    step = SPAN * BLOCK
    sub = lax.broadcasted_iota(jnp.int32, (step, LANES), 0)
    tok = lax.broadcasted_iota(jnp.int32, (step, LANES), 1) // GROUP
    ahead = sub - tok
    lane = lax.broadcasted_iota(jnp.int32, (NB, WIDTH), 1)

    def scores(j, qb):
        rows = ks[pl.ds(pl.multiple_of(j * step, step), step), :]
        return dot(rows, qb, NT)

    def maxima(s):
        return jnp.max(jnp.max(s.reshape(SPAN, BLOCK // 8, 8, LANES), axis=1), axis=1)

    def total(s, m):
        return jnp.sum(jnp.exp2((s - m) * EXP2).reshape(step // 8, 8, LANES), axis=0)

    tgt[...] = jnp.zeros((NB, WIDTH), F32)
    for b in range(LOCAL):
        qb = q_ref[b * LANES : (b + 1) * LANES, :]
        pb = own_sm[b]
        last = pb // SPAN
        bm[...] = jnp.full((NB, LANES), MASKED, F32)

        def masked():
            s = scores(last, qb)
            return jnp.where(ahead > (pb - last * SPAN) * BLOCK, MASKED, s)

        s = masked()
        top = maxima(s)
        bm[pl.ds(pl.multiple_of(last * SPAN, SPAN), SPAN), :] = top
        ref = jnp.max(top, axis=0, keepdims=True)
        acc = total(s, ref)

        def one(j, acc):
            s = scores(j, qb)
            bm[pl.ds(pl.multiple_of(j * SPAN, SPAN), SPAN), :] = maxima(s)
            return acc + total(s, ref)

        acc = lax.fori_loop(0, last, one, acc)
        rmax = jnp.max(bm[...], axis=0, keepdims=True)
        fine = jnp.max((rmax - ref) * EXP2) <= 80.0

        def again():
            def more(j, acc):
                return acc + total(scores(j, qb), rmax)

            return lax.fori_loop(0, last, more, total(masked(), rmax)), rmax

        acc, ref = lax.cond(fine, lambda: (acc, ref), again)
        logsum = jnp.log2(jnp.sum(acc, axis=0, keepdims=True))
        d = (bm[...] - ref) * EXP2 - logsum
        e = d[:, :WIDTH]
        for i in range(1, LANES // WIDTH):
            e = jnp.maximum(e, d[:, i * WIDTH : (i + 1) * WIDTH])
        for shift in (8, 16, 32, 64):
            e = jnp.maximum(e, pltpu.roll(e, shift, 1))
        tgt[...] = jnp.where(lane // GROUP == b, jnp.exp2(e), tgt[...])

    live = lane < LOCAL * GROUP
    pooled = tgt[...]
    psum = jnp.sum(pooled, axis=0, keepdims=True)
    target = jnp.where(live, pooled / jnp.where(psum > 0, psum, 1.0), 0.0)

    extra = gathered_ref[:, ROWS:, :].reshape(SEQ * 16, WIDTH)
    place = lax.broadcasted_iota(jnp.int32, (NB, SEQ * 16), 0)
    kproj = jnp.zeros((NB, WIDTH), F32)
    for i in range(3):
        pick = jnp.where(place == place_ref[i : i + 1, :], 1.0, 0.0).astype(BF16)
        part = dot(pick, extra).astype(BF16)
        kpool_ref[:, i * WIDTH : (i + 1) * WIDTH] = part
        kproj = kproj + dot(part, wk_ref[i * WIDTH : (i + 1) * WIDTH, :])

    q = q_ref[...].astype(F32).reshape(LOCAL, BLOCK, GROUP, WIDTH)
    qpool = (jnp.sum(q, axis=1) * (1.0 / BLOCK)).reshape(LOCAL * GROUP, WIDTH)
    qpool = jnp.concatenate([qpool, jnp.zeros((WIDTH - LOCAL * GROUP, WIDTH), F32)], axis=0)
    qpool = qpool.astype(BF16)
    qproj = dot(qpool, wq_ref[...])

    logits = dot(kproj, qproj, NT, HIGH) * SCALE
    row = lax.broadcasted_iota(jnp.int32, (NB, WIDTH), 0)
    logits = jnp.where(row > ownrow_ref[0:1, :], -1e30, logits)
    shifted = logits - jnp.max(logits, axis=0, keepdims=True)
    ex = jnp.exp(shifted)
    exsum = jnp.sum(ex, axis=0, keepdims=True)
    logp = shifted - jnp.log(exsum)
    scale = 1.0 / (8 * GROUP * NB)
    safe = jnp.log(jnp.where(target > 0, target, 1.0))
    terms = jnp.where(target > 0, target * (safe - logp), 0.0)
    loss = jnp.sum(jnp.sum(terms, axis=0, keepdims=True), axis=1, keepdims=True) * scale
    rowtot = jnp.sum(target, axis=0, keepdims=True)
    dlogit = jnp.where(live, (jnp.exp(logp) * rowtot - target) * (scale * SCALE), 0.0)
    dqproj = dot(dlogit.T, kproj, NN, HIGH)
    dkproj = dot(dlogit, qproj, NN, HIGH)
    gradq = dot(qpool.astype(F32).T, dqproj, NN, HIGH)
    half = SEQ // 2
    out_ref[:half, :8, :] = gradq.reshape(half, 8, WIDTH)
    out_ref[half:, :8, :] = dkproj.reshape(half, 8, WIDTH)
    out_ref[:, 8:, :] = jnp.broadcast_to(loss.reshape(1, 1, 1), (SEQ, 8, WIDTH))


def finish(kpool_ref, dk_ref, out_ref):
    out_ref[...] = dot(kpool_ref[...].astype(F32).T, dk_ref[...], NN, HIGH)


VMEM = pl.BlockSpec(memory_space=pltpu.VMEM)
SMEM = pl.BlockSpec(memory_space=pltpu.SMEM)


def shards(queries, keys, block_order, gate_query, gate_key):
    posrows = jnp.broadcast_to(block_order.astype(F32)[:, None], (LOCAL, WIDTH))
    mine = pl.pallas_call(
        prepare,
        out_shape=jax.ShapeDtypeStruct((8, SENT, WIDTH), BF16),
        in_specs=[VMEM, VMEM],
        out_specs=VMEM,
        name="prepare",
    )(keys.reshape(ROWS, WIDTH), posrows)
    column = lax.all_to_all(mine, "z", 0, 0)
    column = jnp.broadcast_to(column[None], (4, 8, SENT, WIDTH))
    gathered = lax.all_to_all(column, "x", 0, 0).reshape(SEQ, SENT, WIDTH)

    pos = gathered[:, ROWS + 12 :, 0].astype(jnp.int32)
    place = jnp.stack(
        [jnp.pad(pos, ((0, 0), (4 * i, 12 - 4 * i)), constant_values=-1) for i in range(3)]
    ).reshape(3, SEQ * 16)
    ownrow = jnp.pad(jnp.repeat(block_order, GROUP), (0, WIDTH - LOCAL * GROUP))[None]
    sums, kpool = pl.pallas_call(
        attend,
        out_shape=(
            jax.ShapeDtypeStruct((SEQ, 16, WIDTH), F32),
            jax.ShapeDtypeStruct((NB, 3 * WIDTH), BF16),
        ),
        in_specs=[SMEM, SMEM, VMEM, VMEM, VMEM, VMEM, VMEM, VMEM],
        out_specs=(VMEM, VMEM),
        scratch_shapes=[
            pltpu.VMEM((NB * BLOCK, WIDTH), BF16),
            pltpu.VMEM((NB, LANES), F32),
            pltpu.VMEM((NB, WIDTH), F32),
        ],
        compiler_params=pltpu.CompilerParams(vmem_limit_bytes=40 << 20),
        name="attend",
    )(
        pos.reshape(NB), block_order, place, ownrow, gathered,
        queries.reshape(ROWS * GROUP, WIDTH), gate_query[0], gate_key[0],
    )
    got = jnp.sum(lax.all_to_all(sums, ("x", "z"), 0, 0), axis=0)
    loss = lax.psum(got[8, 0], ("y", "core"))
    whole = lax.all_to_all(jnp.broadcast_to(got[None, :8], (SEQ, 8, WIDTH)), ("x", "z"), 0, 0)
    whole = whole.reshape(2, NB, WIDTH)
    grad_k = pl.pallas_call(
        finish,
        out_shape=jax.ShapeDtypeStruct((3 * WIDTH, WIDTH), F32),
        in_specs=[VMEM, VMEM],
        out_specs=VMEM,
        name="finish",
    )(kpool, whole[1])
    return loss, whole[0][None], grad_k[None]


def solution(mesh):
    fine = Mesh(mesh.devices.reshape(4, 8, 4, 2), ("x", "z", "y", "core"))
    seq, head = ("x", "z"), ("y", "core")
    return jax.shard_map(
        shards,
        mesh=fine,
        in_specs=(
            P(seq, head, None),
            P(seq, head, None),
            P(seq),
            P(head, None, None),
            P(head, None, None),
        ),
        out_specs=(P(), P(head, None, None), P(head, None, None)),
        check_vma=False,
    )
```

```python
import functools
import math

import jax
import jax.numpy as jnp
from jax import lax
from jax.experimental import pallas as pl
from jax.experimental.pallas import tpu as pltpu
from jax.sharding import Mesh, PartitionSpec as P

BLOCK = 64
WIDTH = 128
GROUP = 8
LOCAL = 4
NX, NZ = 4, 8
SEQ = NX * NZ
NB = LOCAL * SEQ
ROWS = LOCAL * BLOCK
MORE = ROWS + 16
SENT = MORE + LOCAL * GROUP
LANES = BLOCK * GROUP
PER = LOCAL * NX
QROWS = LOCAL * GROUP
SCALE = WIDTH ** -0.5
EXP2 = SCALE * math.log2(math.e)
MASKED = -1e30 * WIDTH ** 0.5
FAR = 1e30
SHARE = 1.0 / (8 * GROUP * NB)
HIGH = lax.Precision.HIGHEST
NT = (((1,), (1,)), ((), ()))
NN = (((1,), (0,)), ((), ()))
F32 = jnp.float32
BF16 = jnp.bfloat16
VMEM = pl.BlockSpec(memory_space=pltpu.VMEM)
SMEM = pl.BlockSpec(memory_space=pltpu.SMEM)
ANY = pl.BlockSpec(memory_space=pl.ANY)


def dot(a, b, dims=NN, precision=None):
    return lax.dot_general(a, b, dims, precision=precision, preferred_element_type=F32)


def prepare(own_sm, keys_ref, q_ref, out_ref, qpool_ref):
    keys = keys_ref[...]
    blocks = keys.astype(F32)
    kmax = jnp.max(blocks, axis=1)
    kmin = jnp.min(blocks, axis=1)
    kmean = jnp.sum(blocks, axis=1) * (1.0 / BLOCK)
    spot = lax.broadcasted_iota(jnp.int32, (LOCAL, WIDTH), 0)
    pos = jnp.zeros((LOCAL, WIDTH), F32)
    for b in range(LOCAL):
        pos = jnp.where(spot == b, own_sm[b].astype(F32), pos)
    q = q_ref[...].astype(F32).reshape(LOCAL, BLOCK, GROUP, WIDTH)
    qpool = (jnp.sum(q, axis=1) * (1.0 / BLOCK)).reshape(LOCAL * GROUP, WIDTH)
    extra = jnp.concatenate([kmax, kmin, kmean, pos], axis=0).astype(BF16)
    for i in range(NX):
        out_ref[i, :ROWS, :] = keys.reshape(ROWS, WIDTH)
        out_ref[i, ROWS:MORE, :] = extra
        out_ref[i, MORE:, :] = qpool.astype(BF16)
    qpool_ref[...] = qpool.astype(BF16)


def wide(row):
    return jnp.concatenate([row] * (LANES // WIDTH), axis=1)


def fold(rows, qb, pb, ref, acc, keep):
    for r, row in enumerate(rows):
        tops = []
        for i in range(NX):
            s = dot(row[i, :ROWS, :], qb, NT).reshape(LOCAL, BLOCK // 8, 8, LANES)
            pos = row[i, ROWS:MORE, :].astype(F32)
            for j in range(LOCAL):
                at = wide(pos[12 + j : 13 + j, :])
                top = jnp.max(jnp.max(s[j], axis=0), axis=0, keepdims=True)
                tops.append(jnp.where(at < pb, top, jnp.where(at == pb, ref, MASKED)))
                base = ref + jnp.where(at < pb, 0.0, FAR)
                acc = acc + jnp.sum(jnp.exp2((s[j] - base) * EXP2), axis=0)
            if i % 2:
                keep(r * PER + (i - 1) * LOCAL, jnp.concatenate(tops, axis=0))
                tops = []
    return acc


def first(own_sm, keys_ref, q_ref, row, bm_ref, acc_ref, ref_ref):
    sub = lax.broadcasted_iota(jnp.int32, (BLOCK, LANES), 0)
    tok = lax.broadcasted_iota(jnp.int32, (BLOCK, LANES), 1) // GROUP

    def one(b, _):
        qb = q_ref[b]
        s = jnp.where(sub > tok, MASKED, dot(keys_ref[b], qb, NT))
        ref = jnp.max(s, axis=0, keepdims=True)
        acc = jnp.sum(jnp.exp2((s - ref) * EXP2).reshape(BLOCK // 8, 8, LANES), axis=0)
        ref_ref[b] = jnp.broadcast_to(ref, (8, LANES))

        def keep(at, tops):
            bm_ref[b, at : at + 8, :] = tops

        acc_ref[b] = fold([row], qb, own_sm[b].astype(F32), ref, acc, keep)
        return 0

    lax.fori_loop(0, LOCAL, one, 0)


def middle(own_sm, q_ref, ref_ref, acc_in, back, ahead, bm_ref, acc_ref):
    def one(b, _):
        def keep(at, tops):
            bm_ref[b, at : at + 8, :] = tops

        acc_ref[b] = fold(
            [back, ahead], q_ref[b], own_sm[b].astype(F32), ref_ref[b, :1, :], acc_in[b], keep
        )
        return 0

    lax.fori_loop(0, LOCAL, one, 0)


def places(z):
    return [pl.multiple_of(lax.rem(z + off, NZ) * PER, PER) for off in (0, 7, 1, 6, 2, 5, 3, 4)]


def pooled_keys(parts, hs, z, kall):
    for h, at in zip(hs, places(z)):
        tiles = [h[i, ROWS:MORE, :].astype(F32) for i in range(NX)]
        for part in parts:
            got = jnp.concatenate([t[4 * part : 4 * part + 4, :] for t in tiles], axis=0)
            kall[part, pl.ds(at, PER), :] = got


def project(kall, wk_ref):
    kproj = jnp.zeros((NB, WIDTH), F32)
    for part in range(3):
        kproj = kproj + dot(kall[part].astype(BF16), wk_ref[part * WIDTH : (part + 1) * WIDTH, :])
    return kproj


def targets(
    own_sm, z_sm, q_ref, ref_ref, acc_in, last, bm0, bm1, bm2, bm3,
    h0, h1, h2, h3, h4, h5, h6, h7, wq_ref, wk_ref,
    own_ref, out_ref, bm4, acc_s, rmax_s, tgt, kall, held, sem,
):
    rows = (h0, h1, h2, h3, h4, h5, h6, h7)
    z = z_sm[0]

    def one(b, worst):
        def keep(at, tops):
            bm4[b, at : at + 8, :] = tops

        ref = ref_ref[b, :1, :]
        acc_s[b] = fold([last], q_ref[b], own_sm[b].astype(F32), ref, acc_in[b], keep)
        rmax = ref
        for bm in (bm0, bm1, bm2, bm3, bm4):
            rmax = jnp.maximum(rmax, jnp.max(bm[b], axis=0, keepdims=True))
        rmax_s[b] = jnp.broadcast_to(rmax, (8, LANES))
        return jnp.maximum(worst, (rmax - ref) * EXP2)

    worst = lax.fori_loop(0, LOCAL, one, jnp.zeros((1, LANES), F32))
    fine = jnp.max(worst) <= 80.0

    @pl.when(fine)
    def _():
        rmax_s[...] = ref_ref[...]

    @pl.when(jnp.logical_not(fine))
    def _():
        for i, h in enumerate(rows):
            copy = pltpu.make_async_copy(h, held.at[pl.ds(i * NX, NX)], sem)
            copy.start()
            copy.wait()
        acc_s[...] = jnp.zeros((LOCAL, 8, LANES), F32)
        sub = lax.broadcasted_iota(jnp.int32, (BLOCK, LANES), 0).astype(F32)
        tok = (lax.broadcasted_iota(jnp.int32, (BLOCK, LANES), 1) // GROUP).astype(F32)

        def again(i, _):
            pos = held[i, ROWS:MORE, :].astype(F32)
            for j in range(LOCAL):
                at = wide(pos[12 + j : 13 + j, :]) * BLOCK
                keys = held[i, j * BLOCK : (j + 1) * BLOCK, :]
                for b in range(LOCAL):
                    s = dot(keys, q_ref[b], NT)
                    late = at + sub > (own_sm[b] * BLOCK).astype(F32) + tok
                    e = jnp.where(late, 0.0, jnp.exp2((s - rmax_s[b, :1, :]) * EXP2))
                    acc_s[b] = acc_s[b] + jnp.sum(e.reshape(BLOCK // 8, 8, LANES), axis=0)
            return 0

        lax.fori_loop(0, SEQ, again, 0)

    lane = lax.broadcasted_iota(jnp.int32, (PER, WIDTH), 1)
    tgt[...] = jnp.zeros((NB, WIDTH), F32)
    at = places(z)
    parts = [(bm0, 0, at[0]), (bm4, 0, at[7])]
    for k, bm in ((1, bm1), (2, bm2), (3, bm3)):
        parts += [(bm, 0, at[2 * k - 1]), (bm, PER, at[2 * k])]
    for b in range(LOCAL):
        ref = rmax_s[b, :1, :]
        logsum = jnp.log2(jnp.sum(acc_s[b], axis=0, keepdims=True))
        for bm, start, to in parts:
            d = (bm[b, start : start + PER, :] - ref) * EXP2 - logsum
            e = d[:, :WIDTH]
            for i in range(1, LANES // WIDTH):
                e = jnp.maximum(e, d[:, i * WIDTH : (i + 1) * WIDTH])
            for shift in (8, 16, 32, 64):
                e = jnp.maximum(e, pltpu.roll(e, shift, 1))
            tgt[pl.ds(to, PER), :] = jnp.where(lane // GROUP == b, jnp.exp2(e), tgt[pl.ds(to, PER), :])
    pooled = tgt[...].T[: LOCAL * GROUP, :]
    target = pooled / jnp.sum(pooled, axis=1, keepdims=True)

    pooled_keys(range(4), rows, z, kall)
    qproj = dot(own_ref[...], wq_ref[...])
    logits = dot(qproj, project(kall, wk_ref), NT, HIGH) * SCALE
    posr = jnp.concatenate(
        [jnp.full((GROUP, WIDTH), own_sm[b].astype(F32), F32) for b in range(LOCAL)], axis=0
    )
    logits = jnp.where(kall[3].T[:1, :] > posr, -1e30, logits)
    shifted = logits - jnp.max(logits, axis=1, keepdims=True)
    ex = jnp.exp(shifted)
    exsum = jnp.sum(ex, axis=1, keepdims=True)
    logp = shifted - jnp.log(exsum)
    safe = jnp.log(jnp.where(target > 0, target, 1.0))
    terms = jnp.where(target > 0, target * (safe - logp), 0.0)
    loss = jnp.sum(jnp.sum(terms, axis=0, keepdims=True), axis=1, keepdims=True) * SHARE
    rowtot = jnp.sum(target, axis=1, keepdims=True)
    dlogit = (jnp.exp(logp) * rowtot - target) * (SHARE * SCALE)
    mine = jnp.concatenate([dlogit, jnp.broadcast_to(loss, (8, WIDTH))], axis=0)
    for i in range(SEQ):
        out_ref[i] = mine


def finish(
    z_sm, got_ref, h0, h1, h2, h3, h4, h5, h6, h7, wq_ref, wk_ref, gq_ref, gk_ref, qall, kall
):
    rows = (h0, h1, h2, h3, h4, h5, h6, h7)
    z = z_sm[0]
    for h, at in zip(rows, places(z)):
        for i in range(NX):
            to = pl.multiple_of(i * NZ * QROWS + at * (QROWS // PER), QROWS)
            qall[pl.ds(to, QROWS), :] = h[i, MORE:, :]
    pooled_keys(range(3), rows, z, kall)
    kproj = project(kall, wk_ref)
    dlogit = got_ref[:, :QROWS, :].reshape(SEQ * QROWS, WIDTH)
    both = dot(qall[...].astype(F32).T, dlogit, NN, HIGH)
    gq_ref[...] = dot(both, kproj, NN, HIGH)
    dkproj = dot(wq_ref[...].astype(F32).T, both, NN, HIGH)
    for part in range(3):
        out = dot(kall[part].T, dkproj, NT, HIGH)
        gk_ref[part * WIDTH : (part + 1) * WIDTH, :] = out


def call(kernel, out_shape, in_specs, cost, *args, scratch=()):
    return pl.pallas_call(
        kernel,
        out_shape=out_shape,
        in_specs=in_specs,
        out_specs=jax.tree.map(lambda _: VMEM, out_shape),
        scratch_shapes=scratch,
        compiler_params=pltpu.CompilerParams(vmem_limit_bytes=40 << 20),
        cost_estimate=pl.CostEstimate(flops=cost, bytes_accessed=1 << 20, transcendentals=0),
        name=kernel.__name__,
    )(*args)


def whole(shape):
    return pl.BlockSpec(shape, lambda *_: (0,) * len(shape))


def shards(queries, keys, block_order, gate_query, gate_key):
    def f32(*shape):
        return jax.ShapeDtypeStruct(shape, F32)

    own = block_order
    q4 = queries.reshape(LOCAL, LANES, WIDTH)
    k4 = keys.reshape(LOCAL, BLOCK, WIDTH)
    z = lax.axis_index("z").astype(jnp.int32).reshape(1)
    sent = jax.ShapeDtypeStruct((NX, SENT, WIDTH), BF16)
    pooled = jax.ShapeDtypeStruct((QROWS, WIDTH), BF16)
    mine, qpool = pl.pallas_call(
        prepare,
        out_shape=(sent, pooled),
        grid_spec=pltpu.PrefetchScalarGridSpec(
            num_scalar_prefetch=1,
            grid=(1,),
            in_specs=[whole(k4.shape), whole(q4.shape)],
            out_specs=(whole(sent.shape), whole(pooled.shape)),
        ),
        compiler_params=pltpu.CompilerParams(vmem_limit_bytes=40 << 20),
        name="prepare",
    )(own, k4, q4)
    row = lax.all_to_all(mine, "x", 0, 0)

    def shift(a, by):
        return lax.ppermute(a, "z", [(i, (i + by) % NZ) for i in range(NZ)])

    work = 2 * LOCAL * LANES * PER * BLOCK * WIDTH
    state = f32(LOCAL, 8, LANES)
    back, ahead = shift(row, 1), shift(row, -1)
    bm, acc, ref = call(
        first, (f32(LOCAL, PER, LANES), state, state), [SMEM, VMEM, VMEM, VMEM], work,
        own, k4, q4, row,
    )
    bms, rows = [bm], [row]
    for k in range(1, 4):
        rows += [back, ahead]
        back, ahead, acc = lax.optimization_barrier((back, ahead, acc))
        here = (back, ahead)
        back = shift(back, 1)
        ahead = shift(ahead, -1) if k < 3 else None
        bm, acc = call(
            middle, (f32(LOCAL, 2 * PER, LANES), state), [SMEM] + [VMEM] * 5, 2 * work,
            own, q4, ref, acc, *here,
        )
        bms.append(bm)
    rows.append(back)
    spread = call(
        targets, f32(SEQ, QROWS + 8, WIDTH), [SMEM] * 2 + [VMEM] * 19, work,
        own, z, q4, ref, acc, back, *bms, *rows, gate_query[0], gate_key[0], qpool,
        scratch=[
            pltpu.VMEM((LOCAL, PER, LANES), F32),
            pltpu.VMEM((LOCAL, 8, LANES), F32),
            pltpu.VMEM((LOCAL, 8, LANES), F32),
            pltpu.VMEM((NB, WIDTH), F32),
            pltpu.VMEM((4, NB, WIDTH), F32),
            pltpu.VMEM((SEQ, SENT, WIDTH), BF16),
            pltpu.SemaphoreType.DMA,
        ],
    )
    got = lax.all_to_all(spread, ("x", "z"), 0, 0)
    loss = jnp.sum(got[:, QROWS:, :], axis=0)
    loss = lax.all_to_all(jnp.broadcast_to(loss[None], (8, 8, WIDTH)), ("y", "core"), 0, 0)
    grad_q, grad_k = call(
        finish, (f32(WIDTH, WIDTH), f32(3 * WIDTH, WIDTH)), [SMEM] + [VMEM] * 11, work // 4,
        z, got, *rows, gate_query[0], gate_key[0],
        scratch=[pltpu.VMEM((SEQ * QROWS, WIDTH), BF16), pltpu.VMEM((3, NB, WIDTH), F32)],
    )
    return jnp.sum(loss[:, 0, 0]), grad_q[None], grad_k[None]


def solution(mesh):
    fine = Mesh(mesh.devices.reshape(NX, NZ, 4, 2), ("x", "z", "y", "core"))
    seq, head = ("x", "z"), ("y", "core")
    return jax.shard_map(
        shards,
        mesh=fine,
        in_specs=(
            P(seq, head, None),
            P(seq, head, None),
            P(seq),
            P(head, None, None),
            P(head, None, None),
        ),
        out_specs=(P(), P(head, None, None), P(head, None, None)),
        check_vma=False,
    )
```

```python
import functools
import math

import jax
import jax.numpy as jnp
from jax import lax
from jax.experimental import pallas as pl
from jax.experimental.pallas import tpu as pltpu
from jax.sharding import Mesh, PartitionSpec as P

BLOCK = 64
WIDTH = 128
GROUP = 8
LOCAL = 4
NX, NZ = 4, 8
SEQ = NX * NZ
NB = LOCAL * SEQ
ROWS = LOCAL * BLOCK
MORE = ROWS + 16
SENT = MORE + LOCAL * GROUP
LANES = BLOCK * GROUP
PER = LOCAL * NX
QROWS = LOCAL * GROUP
SCALE = WIDTH ** -0.5
EXP2 = SCALE * math.log2(math.e)
MASKED = -1e30 * WIDTH ** 0.5
FAR = 1e30
SHARE = 1.0 / (8 * GROUP * NB)
LIFT = 2.0 ** 14
PIECES = 8
HIGH = lax.Precision.HIGHEST
NT = (((1,), (1,)), ((), ()))
NN = (((1,), (0,)), ((), ()))
F32 = jnp.float32
BF16 = jnp.bfloat16
VMEM = pl.BlockSpec(memory_space=pltpu.VMEM)
HBM = pl.BlockSpec(memory_space=pltpu.HBM)


def dot(a, b, dims=NN, precision=None):
    return lax.dot_general(a, b, dims, precision=precision, preferred_element_type=F32)


def prepare(own_hbm, keys_hbm, q_hbm, out_ref, qpool_ref, own_ref, own_sm, keys_ref, q_ref, sems):
    copies = [
        pltpu.make_async_copy(own_hbm, own_sm, sems.at[0]),
        pltpu.make_async_copy(keys_hbm, keys_ref, sems.at[1]),
        pltpu.make_async_copy(q_hbm, q_ref, sems.at[2]),
    ]
    for copy in copies:
        copy.start()
    for copy in copies:
        copy.wait()
    keys = keys_ref[...]
    blocks = keys.astype(F32)
    kmax = jnp.max(blocks, axis=1)
    kmin = jnp.min(blocks, axis=1)
    kmean = jnp.sum(blocks, axis=1) * (1.0 / BLOCK)
    for b in range(LOCAL):
        own_ref[b] = jnp.full((8, WIDTH), own_sm[b].astype(F32), F32)
    pos = jnp.concatenate([own_ref[b, :1, :] for b in range(LOCAL)], axis=0)
    q = q_ref[...].astype(F32).reshape(LOCAL, BLOCK, GROUP, WIDTH)
    qpool = (jnp.sum(q, axis=1) * (1.0 / BLOCK)).reshape(QROWS, WIDTH).astype(BF16)
    extra = jnp.concatenate([kmax, kmin, kmean, pos], axis=0).astype(BF16)
    for i in range(NX):
        out_ref[i, :ROWS, :] = keys.reshape(ROWS, WIDTH)
        out_ref[i, ROWS:MORE, :] = extra
        out_ref[i, MORE:, :] = qpool
    qpool_ref[...] = qpool


def wide(row):
    return jnp.concatenate([row] * (LANES // WIDTH), axis=1)


def maxima(parts):
    row = lax.broadcasted_iota(jnp.int32, parts[0].shape, 0)
    step = 1
    while len(parts) > 1:
        low = (row // step) % 2 == 0
        parts = [
            jnp.maximum(jnp.where(low, a, b), pltpu.roll(jnp.where(low, b, a), 8 - step, 0))
            for a, b in zip(parts[::2], parts[1::2])
        ]
        step *= 2
    return parts[0]


def fold(rows, qb, pb, ref, acc, keep):
    for r, row in enumerate(rows):
        for i0 in range(0, NX, 2):
            tiles = [row[i, ROWS:MORE, :].astype(F32)[12:, :] for i in (i0, i0 + 1)]
            pos = jnp.concatenate(tiles, axis=0)
            early, same = pos < pb, pos == pb
            off = jnp.where(early, 0.0, FAR)
            offs = [jnp.broadcast_to(off[j : j + 1, :], (8, WIDTH)) for j in range(8)]
            kept, sums = [], []
            for at in range(0, LANES, 256):
                n = 256 // WIDTH
                base = ref[:, at : at + 256]
                tops = []
                total = acc[:, at : at + 256]
                for i in (0, 1):
                    s = dot(row[i0 + i, :ROWS, :], qb[at : at + 256, :], NT)
                    s = s.reshape(LOCAL, BLOCK // 8, 8, 256)
                    for j in range(LOCAL):
                        tops.append(jnp.max(s[j], axis=0))
                        shift = base + jnp.concatenate([offs[i * LOCAL + j]] * n, axis=1)
                        total = total + jnp.sum(jnp.exp2((s[j] - shift) * EXP2), axis=0)
                sums.append(total)
                top = maxima(tops)
                own = jnp.where(jnp.concatenate([same] * n, axis=1), base, MASKED)
                kept.append(jnp.where(jnp.concatenate([early] * n, axis=1), top, own))
            acc = jnp.concatenate(sums, axis=1)
            keep(r * PER + i0 * LOCAL, jnp.concatenate(kept, axis=1))
    return acc


def first(own_ref, keys_ref, q_ref, row, bm_ref, acc_ref, ref_ref):
    sub = lax.broadcasted_iota(jnp.int32, (BLOCK, LANES), 0)
    tok = lax.broadcasted_iota(jnp.int32, (BLOCK, LANES), 1) // GROUP

    def one(b, _):
        qb = q_ref[b]
        s = jnp.where(sub > tok, MASKED, dot(keys_ref[b], qb, NT))
        ref = jnp.broadcast_to(jnp.max(s, axis=0, keepdims=True), (8, LANES))
        acc = jnp.sum(jnp.exp2((s.reshape(BLOCK // 8, 8, LANES) - ref) * EXP2), axis=0)
        ref_ref[b] = ref

        def keep(at, tops):
            bm_ref[b, at : at + 8, :] = tops

        acc_ref[b] = fold([row], qb, own_ref[b], ref, acc, keep)
        return 0

    lax.fori_loop(0, LOCAL, one, 0, unroll=4)


def middle(own_ref, q_ref, ref_ref, acc_in, back, ahead, bm_ref, acc_ref):
    def one(b, _):
        def keep(at, tops):
            bm_ref[b, at : at + 8, :] = tops

        acc_ref[b] = fold(
            [back, ahead], q_ref[b], own_ref[b], ref_ref[b], acc_in[b], keep
        )
        return 0

    lax.fori_loop(0, LOCAL, one, 0, unroll=4)


def places(z):
    return [pl.multiple_of(lax.rem(z + off, NZ) * PER, PER) for off in (0, 7, 1, 6, 2, 5, 3, 4)]


def pooled_keys(parts, hs, z, kall):
    for h, at in zip(hs, places(z)):
        tiles = [h[i, ROWS:MORE, :].astype(F32) for i in range(NX)]
        for part in parts:
            got = jnp.concatenate([t[4 * part : 4 * part + 4, :] for t in tiles], axis=0)
            kall[part, pl.ds(at, PER), :] = got


def project(kall, wk_ref):
    kproj = jnp.zeros((NB, WIDTH), F32)
    for part in range(3):
        kproj = kproj + dot(kall[part].astype(BF16), wk_ref[part * WIDTH : (part + 1) * WIDTH, :])
    return kproj


def places_in(shape):
    row = lax.broadcasted_iota(jnp.int32, shape, len(shape) - 2)
    return row, lax.broadcasted_iota(jnp.int32, shape, len(shape) - 1)


def piece_scale(r):
    return 2.0 ** (12 * r - 64)


def targets(
    own_ref, q_ref, ref_ref, acc_in, last, bm0, bm1, bm2, bm3,
    h0, h1, h2, h3, h4, h5, h6, h7, wq_ref, wk_ref,
    qpool_ref, out_ref, bm4, acc_s, rmax_s, tgt, kall, held, sem,
):
    rows = (h0, h1, h2, h3, h4, h5, h6, h7)
    z = lax.axis_index("z")

    def one(b, worst):
        def keep(at, tops):
            bm4[b, at : at + 8, :] = tops

        ref = ref_ref[b]
        acc_s[b] = fold([last], q_ref[b], own_ref[b], ref, acc_in[b], keep)
        rmax = ref
        for bm in (bm0, bm1, bm2, bm3, bm4):
            rmax = jnp.maximum(rmax, jnp.max(bm[b], axis=0, keepdims=True))
        rmax_s[b] = rmax
        return jnp.maximum(worst, (rmax - ref) * EXP2)

    worst = lax.fori_loop(0, LOCAL, one, jnp.zeros((8, LANES), F32))
    fine = jnp.max(worst) <= 80.0

    @pl.when(fine)
    def _():
        rmax_s[...] = ref_ref[...]

    @pl.when(jnp.logical_not(fine))
    def _():
        for i, h in enumerate(rows):
            copy = pltpu.make_async_copy(h, held.at[pl.ds(i * NX, NX)], sem)
            copy.start()
            copy.wait()
        acc_s[...] = jnp.zeros((LOCAL, 8, LANES), F32)
        sub = lax.broadcasted_iota(jnp.int32, (BLOCK, LANES), 0).astype(F32)
        tok = (lax.broadcasted_iota(jnp.int32, (BLOCK, LANES), 1) // GROUP).astype(F32)

        def again(i, _):
            pos = held[i, ROWS:MORE, :].astype(F32)
            for j in range(LOCAL):
                at = wide(pos[12 + j : 13 + j, :]) * BLOCK
                keys = held[i, j * BLOCK : (j + 1) * BLOCK, :]
                for b in range(LOCAL):
                    s = dot(keys, q_ref[b], NT)
                    late = at + sub > wide(own_ref[b, :1, :]) * BLOCK + tok
                    e = jnp.where(late, 0.0, jnp.exp2((s - rmax_s[b, :1, :]) * EXP2))
                    acc_s[b] = acc_s[b] + jnp.sum(e.reshape(BLOCK // 8, 8, LANES), axis=0)
            return 0

        lax.fori_loop(0, SEQ, again, 0)

    lane = lax.broadcasted_iota(jnp.int32, (PER, WIDTH), 1)
    tgt[...] = jnp.zeros((NB, WIDTH), F32)
    at = places(z)
    parts = [(bm0, 0, at[0]), (bm4, 0, at[7])]
    for k, bm in ((1, bm1), (2, bm2), (3, bm3)):
        parts += [(bm, 0, at[2 * k - 1]), (bm, PER, at[2 * k])]
    for b in range(LOCAL):
        ref = rmax_s[b, :1, :]
        logsum = jnp.log2(jnp.sum(acc_s[b], axis=0, keepdims=True))
        for bm, start, to in parts:
            d = (bm[b, start : start + PER, :] - ref) * EXP2 - logsum
            e = d[:, :WIDTH]
            for i in range(1, LANES // WIDTH):
                e = jnp.maximum(e, d[:, i * WIDTH : (i + 1) * WIDTH])
            for shift in (8, 16, 32, 64):
                e = jnp.maximum(e, pltpu.roll(e, shift, 1))
            tgt[pl.ds(to, PER), :] = jnp.where(lane // GROUP == b, jnp.exp2(e), tgt[pl.ds(to, PER), :])
    pooled = tgt[...].T[: LOCAL * GROUP, :]
    target = pooled / jnp.sum(pooled, axis=1, keepdims=True)

    pooled_keys(range(4), rows, z, kall)
    qproj = dot(qpool_ref[...], wq_ref[...])
    logits = dot(qproj, project(kall, wk_ref), NT, HIGH) * SCALE
    posr = own_ref[...].reshape(QROWS, WIDTH)
    logits = jnp.where(kall[3].T[:1, :] > posr, -1e30, logits)
    shifted = logits - jnp.max(logits, axis=1, keepdims=True)
    ex = jnp.exp(shifted)
    exsum = jnp.sum(ex, axis=1, keepdims=True)
    logp = shifted - jnp.log(exsum)
    safe = jnp.log(jnp.where(target > 0, target, 1.0))
    terms = jnp.where(target > 0, target * (safe - logp), 0.0)
    loss = jnp.sum(jnp.sum(terms, axis=0, keepdims=True), axis=1, keepdims=True) * SHARE
    rowtot = jnp.sum(target, axis=1, keepdims=True)
    dlogit = jnp.exp(logp) * rowtot - target
    dlogit = dlogit * LIFT
    row, col = places_in(dlogit.shape)
    for r in range(PIECES):
        scaled = loss * piece_scale(r)
        piece = jnp.where(jnp.abs(scaled) >= 2.0 ** -14, scaled.astype(BF16).astype(F32), 0.0)
        loss = loss - piece * (1.0 / piece_scale(r))
        dlogit = jnp.where((row == r) & (col == 0), piece, dlogit)
    out_ref[...] = dlogit


def head_loss(got_ref, out_ref):
    got = jnp.sum(got_ref[:, :PIECES, :], axis=0)
    row, col = places_in(got.shape)
    total = jnp.zeros(got.shape, F32)
    for r in range(PIECES):
        total = jnp.where((row == r) & (col == 0), got * (1.0 / piece_scale(r)), total)
    total = jnp.sum(jnp.sum(total, axis=0, keepdims=True), axis=1, keepdims=True)
    out_ref[...] = jnp.broadcast_to(total.reshape(1, 1, 1), out_ref.shape)


def finish(
    got_ref, h0, h1, h2, h3, h4, h5, h6, h7, wq_ref, wk_ref, gq_ref, gk_ref, qall, kall
):
    rows = (h0, h1, h2, h3, h4, h5, h6, h7)
    z = lax.axis_index("z")
    for h, at in zip(rows, places(z)):
        for i in range(NX):
            to = pl.multiple_of(i * NZ * QROWS + at * (QROWS // PER), QROWS)
            qall[pl.ds(to, QROWS), :] = h[i, MORE:, :]
    pooled_keys(range(3), rows, z, kall)
    kproj = project(kall, wk_ref)
    row, col = places_in(got_ref.shape)
    held = (row < PIECES) & (col == 0)
    dlogit = jnp.where(held, 0.0, got_ref[...])
    rest = jnp.sum(dlogit, axis=2, keepdims=True)
    dlogit = jnp.where(held, -rest, dlogit)
    rest = jnp.sum(dlogit, axis=2, keepdims=True)
    size = jnp.sum(jnp.abs(dlogit), axis=2, keepdims=True)
    dlogit = dlogit - jnp.abs(dlogit) * (rest / jnp.where(size > 0, size, 1.0))
    dlogit = dlogit.reshape(SEQ * QROWS, WIDTH) * (SHARE * SCALE / LIFT)
    both = dot(qall[...].astype(F32).T, dlogit, NN, HIGH)
    gq_ref[...] = dot(both, kproj, NN, HIGH)
    dkproj = dot(wq_ref[...].astype(F32).T, both, NN, HIGH)
    for part in range(3):
        out = dot(kall[part].T, dkproj, NT, HIGH)
        gk_ref[part * WIDTH : (part + 1) * WIDTH, :] = out


def call(kernel, out_shape, in_specs, cost, *args, scratch=()):
    return pl.pallas_call(
        kernel,
        out_shape=out_shape,
        in_specs=in_specs,
        out_specs=jax.tree.map(lambda _: VMEM, out_shape),
        scratch_shapes=scratch,
        compiler_params=pltpu.CompilerParams(vmem_limit_bytes=40 << 20),
        cost_estimate=pl.CostEstimate(flops=cost, bytes_accessed=1 << 20, transcendentals=0),
        name=kernel.__name__,
    )(*args)


def shards(queries, keys, block_order, gate_query, gate_key):
    def f32(*shape):
        return jax.ShapeDtypeStruct(shape, F32)

    q4 = queries.reshape(LOCAL, LANES, WIDTH)
    k4 = keys.reshape(LOCAL, BLOCK, WIDTH)
    mine, qpool, own = pl.pallas_call(
        prepare,
        out_shape=(
            jax.ShapeDtypeStruct((NX, SENT, WIDTH), BF16),
            jax.ShapeDtypeStruct((QROWS, WIDTH), BF16),
            f32(LOCAL, 8, WIDTH),
        ),
        in_specs=[HBM] * 3,
        out_specs=(VMEM, VMEM, VMEM),
        scratch_shapes=[
            pltpu.SMEM((LOCAL,), jnp.int32),
            pltpu.VMEM(k4.shape, BF16),
            pltpu.VMEM(q4.shape, BF16),
            pltpu.SemaphoreType.DMA((3,)),
        ],
        name="prepare",
    )(block_order, k4, q4)
    row = lax.all_to_all(mine, "x", 0, 0)

    def shift(a, by):
        return lax.ppermute(a, "z", [(i, (i + by) % NZ) for i in range(NZ)])

    work = 2 * LOCAL * LANES * PER * BLOCK * WIDTH
    state = f32(LOCAL, 8, LANES)
    back, ahead = shift(row, 1), shift(row, -1)
    bm, acc, ref = call(
        first, (f32(LOCAL, PER, LANES), state, state), [VMEM] * 4, work,
        own, k4, q4, row,
    )
    bms, rows = [bm], [row]
    for k in range(1, 4):
        rows += [back, ahead]
        back, ahead, acc = lax.optimization_barrier((back, ahead, acc))
        here = (back, ahead)
        back = shift(back, 1)
        ahead = shift(ahead, -1) if k < 3 else None
        bm, acc = call(
            middle, (f32(LOCAL, 2 * PER, LANES), state), [VMEM] * 6, 2 * work,
            own, q4, ref, acc, *here,
        )
        bms.append(bm)
    rows.append(back)
    dlogit = call(
        targets, f32(QROWS, WIDTH), [VMEM] * 20, work,
        own, q4, ref, acc, back, *bms, *rows, gate_query[0], gate_key[0], qpool,
        scratch=[
            pltpu.VMEM((LOCAL, PER, LANES), F32),
            pltpu.VMEM((LOCAL, 8, LANES), F32),
            pltpu.VMEM((LOCAL, 8, LANES), F32),
            pltpu.VMEM((NB, WIDTH), F32),
            pltpu.VMEM((4, NB, WIDTH), F32),
            pltpu.VMEM((SEQ, SENT, WIDTH), BF16),
            pltpu.SemaphoreType.DMA,
        ],
    )
    spread = jnp.broadcast_to(dlogit.astype(jnp.float16)[None], (SEQ, QROWS, WIDTH))
    got = lax.all_to_all(spread, ("x", "z"), 0, 0).astype(F32)
    loss = call(head_loss, f32(8, 8, WIDTH), [VMEM], 1 << 16, got)
    loss = lax.all_to_all(loss, ("y", "core"), 0, 0)
    grad_q, grad_k = call(
        finish, (f32(WIDTH, WIDTH), f32(3 * WIDTH, WIDTH)), [VMEM] * 11, work // 4,
        got, *rows, gate_query[0], gate_key[0],
        scratch=[pltpu.VMEM((SEQ * QROWS, WIDTH), BF16), pltpu.VMEM((3, NB, WIDTH), F32)],
    )
    return jnp.sum(loss[:, 0, 0]), grad_q[None], grad_k[None]


def solution(mesh):
    fine = Mesh(mesh.devices.reshape(NX, NZ, 4, 2), ("x", "z", "y", "core"))
    seq, head = ("x", "z"), ("y", "core")
    return jax.shard_map(
        shards,
        mesh=fine,
        in_specs=(
            P(seq, head, None),
            P(seq, head, None),
            P(seq),
            P(head, None, None),
            P(head, None, None),
        ),
        out_specs=(P(), P(head, None, None), P(head, None, None)),
        check_vma=False,
    )
```

```python
import functools
import math

import jax
import jax.numpy as jnp
from jax import lax
from jax.experimental import pallas as pl
from jax.experimental.pallas import tpu as pltpu
from jax.sharding import Mesh, PartitionSpec as P

BLOCK = 64
WIDTH = 128
GROUP = 8
LOCAL = 4
NX, NZ = 4, 8
SEQ = NX * NZ
NB = LOCAL * SEQ
ROWS = LOCAL * BLOCK
MORE = ROWS + 16
SENT = MORE + LOCAL * GROUP
LANES = BLOCK * GROUP
HX = NX // 2
HALF = LOCAL * HX
EXTRA = SENT - ROWS
STATS = 4 * LOCAL
CUT = HX * EXTRA * WIDTH // LANES
QSENT = LANES + 16
QROWS = LOCAL * GROUP
SCALE = WIDTH ** -0.5
EXP2 = SCALE * math.log2(math.e)
MASKED = -1e30 * WIDTH ** 0.5
FAR = 1e30
SHARE = 1.0 / (8 * GROUP * NB)
LIFT = 2.0 ** 14
HIGH = lax.Precision.HIGHEST
NT = (((1,), (1,)), ((), ()))
NN = (((1,), (0,)), ((), ()))
F32 = jnp.float32
BF16 = jnp.bfloat16
VMEM = pl.BlockSpec(memory_space=pltpu.VMEM)
HBM = pl.BlockSpec(memory_space=pltpu.HBM)


def dot(a, b, dims=NN, precision=None):
    return lax.dot_general(a, b, dims, precision=precision, preferred_element_type=F32)


def prepare(own_hbm, keys_hbm, q_hbm, out_ref, qx_ref, own_sm, keys_ref, q_ref, sems):
    copies = [
        pltpu.make_async_copy(own_hbm, own_sm, sems.at[0]),
        pltpu.make_async_copy(keys_hbm, keys_ref, sems.at[1]),
        pltpu.make_async_copy(q_hbm, q_ref, sems.at[2]),
    ]
    for copy in copies:
        copy.start()
    for copy in copies:
        copy.wait()
    keys = keys_ref[...]
    blocks = keys.astype(F32)
    kmax = jnp.max(blocks, axis=1)
    kmin = jnp.min(blocks, axis=1)
    kmean = jnp.sum(blocks, axis=1) * (1.0 / BLOCK)
    pos = [jnp.full((1, WIDTH), own_sm[b].astype(F32), F32) for b in range(LOCAL)]
    sub = lax.broadcasted_iota(jnp.int32, (BLOCK, LANES), 0)
    tok = lax.broadcasted_iota(jnp.int32, (BLOCK, LANES), 1) // GROUP
    for b in range(LOCAL):
        s = jnp.where(sub > tok, MASKED, dot(keys[b], q_ref[b], NT))
        ref = jnp.max(s, axis=0, keepdims=True)
        rows = [ref[:, i * WIDTH : (i + 1) * WIDTH] for i in range(LANES // WIDTH)]
        rows += [pos[b], jnp.zeros((11, WIDTH), F32)]
        qx_ref[b, :LANES, :] = q_ref[b]
        qx_ref[b, LANES:, :] = jnp.concatenate(rows, axis=0).astype(BF16)
    pos = jnp.concatenate(pos, axis=0)
    q = q_ref[...].astype(F32).reshape(LOCAL, BLOCK, GROUP, WIDTH)
    qpool = (jnp.sum(q, axis=1) * (1.0 / BLOCK)).reshape(QROWS, WIDTH).astype(BF16)
    extra = jnp.concatenate([kmax, kmin, kmean, pos], axis=0).astype(BF16)
    out_ref[:ROWS, :] = keys.reshape(ROWS, WIDTH)
    out_ref[ROWS:MORE, :] = extra
    out_ref[MORE:, :] = qpool


def maxima(parts):
    row = lax.broadcasted_iota(jnp.int32, parts[0].shape, 0)
    step = 1
    while len(parts) > 1:
        low = (row // step) % 2 == 0
        parts = [
            jnp.maximum(jnp.where(low, a, b), pltpu.roll(jnp.where(low, b, a), 8 - step, 0))
            for a, b in zip(parts[::2], parts[1::2])
        ]
        step *= 2
    return parts[0]


def fold(rows, qb, pb, ref, acc, keep, diag=None):
    for r, row in enumerate(rows):
        for i0 in range(0, HX, 2):
            tiles = [row[i, ROWS:MORE, :].astype(F32)[12:, :] for i in (i0, i0 + 1)]
            pos = jnp.concatenate(tiles, axis=0)
            early, same = pos < pb, pos == pb
            off = jnp.where(early, 0.0, FAR)
            offs = [jnp.broadcast_to(off[j : j + 1, :], (8, WIDTH)) for j in range(8)]
            kept, sums = [], []
            for at in range(0, LANES, 512):
                n = 512 // WIDTH
                base = ref[:, at : at + 512]
                tops = []
                total = acc[:, at : at + 512]
                for i in (0, 1):
                    s = dot(row[i0 + i, :ROWS, :], qb[at : at + 512, :], NT)
                    s = s.reshape(LOCAL, BLOCK // 8, 8, 512)
                    for j in range(LOCAL):
                        tops.append(jnp.max(s[j], axis=0))
                        shift = base + jnp.concatenate([offs[i * LOCAL + j]] * n, axis=1)
                        total = total + jnp.sum(jnp.exp2((s[j] - shift) * EXP2), axis=0)
                sums.append(total)
                top = maxima(tops)
                own = MASKED
                if diag is not None:
                    own = jnp.where(jnp.concatenate([same] * n, axis=1), diag[:, at : at + 512], MASKED)
                kept.append(jnp.where(jnp.concatenate([early] * n, axis=1), top, own))
            acc = jnp.concatenate(sums, axis=1)
            keep(r * HALF, jnp.concatenate(kept, axis=1))
    return acc


def stage(mine, q, mine_ref, q_ref):
    mine_ref[...] = mine[...]
    q_ref[...] = q[...]


def join(mine, beside, out_ref):
    odd = lax.axis_index("x") % 2
    out_ref[odd] = mine[...]
    out_ref[1 - odd] = beside[...]


def start_of(q_ref, b):
    extra = q_ref[b, LANES:, :].astype(F32)
    spread = [jnp.broadcast_to(extra[i : i + 1, :], (8, WIDTH)) for i in range(5)]
    return spread[4], jnp.concatenate(spread[:4], axis=1)


def sweep(*jobs):
    def run(job, b, ref, acc, store):
        rows, q_ref, _, bm_ref, acc_ref, ref_ref, diags = job
        pos, _ = start_of(q_ref, b)
        best = [ref]

        def keep(at, tops):
            best.append(jnp.maximum(best[-1], tops))
            if store:
                bm_ref[b, at : at + 8, :] = tops

        diag = diags[b] if diags is not None else None
        acc_ref[b] = fold(rows, q_ref[b, :LANES, :], pos, ref, acc, keep, diag)
        ref_ref[b] = ref
        return (best[-1] - ref) * EXP2

    worst = jnp.zeros((8, LANES), F32)
    for job in jobs:

        def one(b, worst, job=job):
            return jnp.maximum(worst, run(job, b, *job[2](b), True))

        worst = lax.fori_loop(0, LOCAL, one, worst, unroll=4)

    @pl.when(jnp.max(worst) > 80.0)
    def _():
        for job in jobs:

            def again(b, _, job=job):
                ref, acc = job[2](b)
                high = jnp.maximum(ref, jnp.max(job[3][b], axis=0, keepdims=True))
                run(job, b, high, acc * jnp.exp2((ref - high) * EXP2), False)
                return 0

            lax.fori_loop(0, LOCAL, again, 0)


def held(ref_in, acc_in):
    return lambda b: (ref_in[b], acc_in[b])


def first(q_ref, mine_ref, half, bm_ref, acc_ref, ref_ref, diags):
    sub = lax.broadcasted_iota(jnp.int32, (BLOCK, LANES), 0)
    tok = lax.broadcasted_iota(jnp.int32, (BLOCK, LANES), 1) // GROUP

    def state(b):
        _, ref = start_of(q_ref, b)
        s = jnp.where(sub > tok, MASKED, dot(mine_ref[pl.ds(pl.multiple_of(b * BLOCK, BLOCK), BLOCK), :], q_ref[b, :LANES, :], NT))
        diags[b] = jnp.broadcast_to(jnp.max(s, axis=0, keepdims=True), (8, LANES))
        e = jnp.exp2((s.reshape(BLOCK // 8, 8, LANES) - ref) * EXP2)
        return ref, jnp.sum(e, axis=0)

    sweep(([half], q_ref, state, bm_ref, acc_ref, ref_ref, diags))


def partner_first(q_ref, half, back, ahead, bm_ref, acc_ref, ref_ref):
    def state(b):
        return start_of(q_ref, b)[1], jnp.zeros((8, LANES), F32)

    sweep(([half, back, ahead], q_ref, state, bm_ref, acc_ref, ref_ref, None))


def middle(q_ref, acc_in, ref_in, back, ahead, bm_ref, acc_ref, ref_ref):
    sweep(([back, ahead], q_ref, held(ref_in, acc_in), bm_ref, acc_ref, ref_ref, None))


def both(q0, acc0, ref0, q1, acc1, ref1, back, ahead, bm0, acc0_out, ref0_out, bm1, acc1_out, ref1_out):
    sweep(
        ([back, ahead], q0, held(ref0, acc0), bm0, acc0_out, ref0_out, None),
        ([back, ahead], q1, held(ref1, acc1), bm1, acc1_out, ref1_out, None),
    )


def last_rows(q0, acc0, ref0, q1, acc1, ref1, row, bm0, bm1, stat_ref, a0, r0, a1, r1):
    sweep(
        ([row], q0, held(ref0, acc0), bm0, a0, r0, None),
        ([row], q1, held(ref1, acc1), bm1, a1, r1, None),
    )
    for n, (acc, ref) in enumerate(((a0, r0), (a1, r1))):
        for b in range(LOCAL):
            pair = [jnp.sum(acc[b], axis=0, keepdims=True), ref[b, :1, :]]
            at = (n * LOCAL + b) * 2
            stat_ref[at : at + 2, :] = jnp.concatenate(pair, axis=0)
    extra = row[:, ROWS:, :].astype(F32).reshape(HX * EXTRA, WIDTH)
    wide_rows = [extra[i * CUT : (i + 1) * CUT, :] for i in range(LANES // WIDTH)]
    stat_ref[STATS:, :] = jnp.concatenate(wide_rows, axis=1)


OFFSETS = (0, 7, 1, 6, 2, 5, 3, 4)


def pool(stat, other, *refs):
    bms, (out_ref, tgt) = (refs[:5], refs[5:9]), refs[11:]
    z = lax.axis_index("z")
    lane = lax.broadcasted_iota(jnp.int32, (HALF, WIDTH), 1)
    tgt[...] = jnp.zeros(tgt.shape, F32)
    for n in range(2):
        for b in range(LOCAL):
            here, there = (n * LOCAL + b) * 2, ((1 - n) * LOCAL + b) * 2
            ref0, ref1 = stat[here + 1 : here + 2, :], other[there + 1 : there + 2, :]
            ref = jnp.maximum(ref0, ref1)
            total = stat[here : here + 1, :] * jnp.exp2((ref0 - ref) * EXP2)
            total = total + other[there : there + 1, :] * jnp.exp2((ref1 - ref) * EXP2)
            logsum = jnp.log2(total)
            k = 0
            for bm in bms[n]:
                d = (bm[b] - ref) * EXP2 - logsum
                e = d[:, :WIDTH]
                for i in range(1, LANES // WIDTH):
                    e = jnp.maximum(e, d[:, i * WIDTH : (i + 1) * WIDTH])
                for shift in (8, 16, 32, 64):
                    e = jnp.maximum(e, pltpu.roll(e, shift, 1))
                e = jnp.exp2(e)
                for i in range(bm.shape[1] // HALF):
                    at = pl.multiple_of(lax.rem(z + OFFSETS[k], NZ) * HALF + n * NB // 2, HALF)
                    part = e[i * HALF : (i + 1) * HALF, :]
                    tgt[pl.ds(at, HALF), :] += jnp.where(lane // GROUP == b, part, 0.0)
                    k += 1
    out_ref[...] = tgt[...].T[:QROWS, :] * LIFT


def collect(mine, other, row, stat, qall, kall, posr=None):
    x, z = lax.axis_index("x"), lax.axis_index("z")

    def extra(far, k, i):
        if k < NZ - 1:
            ex = other if far else mine
            return ex[k * HX + i, :16, :].astype(F32), ex[k * HX + i, 16:, :]
        if not far:
            return row[i, ROWS:MORE, :].astype(F32), row[i, MORE:, :]
        low = stat[STATS:, 2 * i * WIDTH : (2 * i + 1) * WIDTH]
        high = stat[STATS:, (2 * i + 1) * WIDTH : (2 * i + 2) * WIDTH]
        return low[:16, :], jnp.concatenate([low[16:, :], high], axis=0).astype(BF16)

    for far, side in ((False, x // 2), (True, 1 - x // 2)):
        for k, off in enumerate(OFFSETS):
            at = lax.rem(z + off, NZ)
            pieces = [extra(far, k, i) for i in range(HX)]
            for part in range(4):
                got = jnp.concatenate([t[4 * part : 4 * part + 4, :] for t, _ in pieces], axis=0)
                to = pl.multiple_of(side * (NB // 2) + at * HALF, HALF)
                kall[part, pl.ds(to, HALF), :] = got
            for i, (tile, queries) in enumerate(pieces):
                to = pl.multiple_of(((side * HX + i) * NZ + at) * QROWS, QROWS)
                qall[pl.ds(to, QROWS), :] = queries
                if posr is not None:
                    rows = [jnp.broadcast_to(tile[12 + b : 13 + b, :], (GROUP, WIDTH)) for b in range(LOCAL)]
                    posr[pl.ds(to, QROWS), :] = jnp.concatenate(rows, axis=0)


def project(kall, wk_ref):
    kproj = jnp.zeros((NB, WIDTH), F32)
    for part in range(3):
        kproj = kproj + dot(kall[part].astype(BF16), wk_ref[part * WIDTH : (part + 1) * WIDTH, :])
    return kproj


def all_targets(got_ref):
    lane = lax.broadcasted_iota(jnp.int32, (NZ * QROWS, WIDTH), 1)
    parts = []
    for x in range(NX):
        own = got_ref[x * NZ : (x + 1) * NZ].reshape(NZ * QROWS, WIDTH)
        far = got_ref[(NX - 1 - x) * NZ : (NX - x) * NZ].reshape(NZ * QROWS, WIDTH)
        row = jnp.where(lane < NB // 2, own, far)
        parts.append(row if x < HX else pltpu.roll(row, NB // 2, 1))
    pooled = jnp.concatenate(parts, axis=0)
    return pooled / jnp.sum(pooled, axis=1, keepdims=True)


def head_loss(got_ref, mine, other, row, stat, wq_ref, wk_ref, out_ref, logp_ref, qall, kall, posr):
    collect(mine, other, row, stat, qall, kall, posr)
    qproj = dot(qall[...], wq_ref[...])
    logits = dot(qproj, project(kall, wk_ref), NT, HIGH) * SCALE
    logits = jnp.where(kall[3].T[:1, :] > posr[...], -1e30, logits)
    shifted = logits - jnp.max(logits, axis=1, keepdims=True)
    logp = shifted - jnp.log(jnp.sum(jnp.exp(shifted), axis=1, keepdims=True))
    logp_ref[...] = logp
    target = all_targets(got_ref)
    safe = jnp.log(jnp.where(target > 0, target, 1.0))
    terms = jnp.where(target > 0, target * (safe - logp), 0.0)
    loss = jnp.sum(jnp.sum(terms, axis=0, keepdims=True), axis=1, keepdims=True) * SHARE
    out_ref[...] = jnp.broadcast_to(loss.reshape(1, 1, 1), out_ref.shape)


def finish(got_ref, logp_ref, mine, other, row, stat, wq_ref, wk_ref, gq_ref, gk_ref, qall, kall):
    collect(mine, other, row, stat, qall, kall)
    target = all_targets(got_ref)
    rowtot = jnp.sum(target, axis=1, keepdims=True)
    dlogit = (jnp.exp(logp_ref[...]) * rowtot - target) * (SHARE * SCALE)
    both = dot(qall[...].astype(F32).T, dlogit, NN, HIGH)
    gq_ref[...] = dot(both, project(kall, wk_ref), NN, HIGH)
    dkproj = dot(wq_ref[...].astype(F32).T, both, NN, HIGH)
    for part in range(3):
        gk_ref[part * WIDTH : (part + 1) * WIDTH, :] = dot(kall[part].T, dkproj, NT, HIGH)


def call(kernel, out_shape, cost, *args, scratch=()):
    return pl.pallas_call(
        kernel,
        out_shape=out_shape,
        in_specs=[VMEM] * len(args),
        out_specs=jax.tree.map(lambda _: VMEM, out_shape),
        scratch_shapes=scratch,
        compiler_params=pltpu.CompilerParams(vmem_limit_bytes=40 << 20),
        cost_estimate=pl.CostEstimate(flops=cost, bytes_accessed=1 << 20, transcendentals=0),
        name=kernel.__name__,
    )(*args)


def shards(queries, keys, block_order, gate_query, gate_key):
    def f32(*shape):
        return jax.ShapeDtypeStruct(shape, F32)

    q4 = queries.reshape(LOCAL, LANES, WIDTH)
    k4 = keys.reshape(LOCAL, BLOCK, WIDTH)
    mine, q0 = pl.pallas_call(
        prepare,
        out_shape=(
            jax.ShapeDtypeStruct((SENT, WIDTH), BF16),
            jax.ShapeDtypeStruct((LOCAL, QSENT, WIDTH), BF16),
        ),
        in_specs=[HBM] * 3,
        out_specs=(VMEM, VMEM),
        scratch_shapes=[
            pltpu.SMEM((LOCAL,), jnp.int32),
            pltpu.VMEM(k4.shape, BF16),
            pltpu.VMEM(q4.shape, BF16),
            pltpu.SemaphoreType.DMA((3,)),
        ],
        name="prepare",
    )(block_order, k4, q4)

    def as_one(a):
        return jax.ShapeDtypeStruct(a.shape, a.dtype)

    def partner(a):
        return lax.ppermute(a, "x", [(i, NX - 1 - i) for i in range(NX)])

    def shift(a, by):
        return lax.ppermute(a, "z", [(i, (i + by) % NZ) for i in range(NZ)])

    beside = lax.ppermute(mine, "x", [(i, i ^ 1) for i in range(NX)])
    q1 = partner(q0)
    mine, q0 = call(stage, (as_one(mine), as_one(q0)), 1 << 10, mine, q0)
    half = call(join, jax.ShapeDtypeStruct((HX, SENT, WIDTH), BF16), 1 << 10, mine, beside)
    unit = LOCAL * LANES * HALF * BLOCK * WIDTH * 2
    state = (f32(LOCAL, 8, LANES),) * 2

    def maxima_of(n):
        return f32(LOCAL, n * HALF, LANES)

    rows = [half]
    back, ahead = shift(half, 1), shift(half, -1)
    bm, acc, ref = call(
        first, (maxima_of(1),) + state, unit, q0, mine, half,
        scratch=[pltpu.VMEM((LOCAL, 8, LANES), F32)],
    )
    own, other = [bm], []
    for k in range(1, 4):
        back, ahead, acc = lax.optimization_barrier((back, ahead, acc))
        here = (back, ahead)
        rows += here
        back = shift(back, 1)
        ahead = shift(ahead, -1) if k < 3 else None
        if k == 3:
            extras = jnp.concatenate([row[:, ROWS:, :] for row in rows], axis=0)
            far_extras = partner(extras)
        if k == 1:
            bm, acc, ref = call(middle, (maxima_of(2),) + state, 2 * unit, q0, acc, ref, *here)
            q1, acc = lax.optimization_barrier((q1, acc))
            bm1, acc1, ref1 = call(partner_first, (maxima_of(3),) + state, 3 * unit, q1, *rows)
        else:
            bm, acc, ref, bm1, acc1, ref1 = call(
                both, ((maxima_of(2),) + state) * 2, 4 * unit, q0, acc, ref, q1, acc1, ref1, *here
            )
        own.append(bm)
        other.append(bm1)
        acc, acc1 = lax.optimization_barrier((acc, acc1))
    bm0, bm1, stat = call(
        last_rows, (maxima_of(1), maxima_of(1), f32(STATS + CUT, LANES)), 2 * unit,
        q0, acc, ref, q1, acc1, ref1, back,
        scratch=[pltpu.VMEM((LOCAL, 8, LANES), F32)] * 4,
    )
    far_stat, far_extras = lax.optimization_barrier((partner(stat), far_extras))
    pooled = call(
        pool, f32(QROWS, WIDTH), unit // 4, stat, far_stat, *own, bm0, *other, bm1,
        gate_query[0], gate_key[0],
        scratch=[pltpu.VMEM((NB, WIDTH), F32)],
    )
    spread = jnp.broadcast_to(pooled.astype(jnp.float16)[None], (SEQ, QROWS, WIDTH))
    given = (extras, far_extras, back, far_stat, gate_query[0], gate_key[0])
    got = lax.all_to_all(spread, ("x", "z"), 0, 0).astype(F32)
    gathered = [pltpu.VMEM((SEQ * QROWS, WIDTH), BF16), pltpu.VMEM((4, NB, WIDTH), F32)]
    loss, logp = call(
        head_loss, (f32(8, 8, WIDTH), f32(SEQ * QROWS, WIDTH)), unit, got, *given,
        scratch=gathered + [pltpu.VMEM((SEQ * QROWS, WIDTH), F32)],
    )
    loss = lax.all_to_all(loss, ("y", "core"), 0, 0)
    grad_q, grad_k = call(
        finish, (f32(WIDTH, WIDTH), f32(3 * WIDTH, WIDTH)), unit,
        got, logp, *given, scratch=gathered,
    )
    return jnp.sum(loss[:, 0, 0]), grad_q[None], grad_k[None]


def solution(mesh):
    fine = Mesh(mesh.devices.reshape(NX, NZ, 4, 2), ("x", "z", "y", "core"))
    seq, head = ("x", "z"), ("y", "core")
    return jax.shard_map(
        shards,
        mesh=fine,
        in_specs=(
            P(seq, head, None),
            P(seq, head, None),
            P(seq),
            P(head, None, None),
            P(head, None, None),
        ),
        out_specs=(P(), P(head, None, None), P(head, None, None)),
        check_vma=False,
    )
```

```python
import functools
import math

import jax
import jax.numpy as jnp
from jax import lax
from jax.experimental import pallas as pl
from jax.experimental.pallas import tpu as pltpu
from jax.sharding import Mesh, PartitionSpec as P

BLOCK = 64
WIDTH = 128
GROUP = 8
LOCAL = 4
NX, NZ = 4, 8
SEQ = NX * NZ
NB = LOCAL * SEQ
ROWS = LOCAL * BLOCK
MORE = ROWS + 16
SENT = MORE + LOCAL * GROUP
LANES = BLOCK * GROUP
HX = NX // 2
HALF = LOCAL * HX
EXTRA = SENT - ROWS
STATS = 4 * LOCAL
CUT = HX * EXTRA * WIDTH // LANES
QSENT = LANES + 16
QROWS = LOCAL * GROUP
SCALE = WIDTH ** -0.5
EXP2 = SCALE * math.log2(math.e)
MASKED = -1e30 * WIDTH ** 0.5
FAR = 1e30
SHARE = 1.0 / (8 * GROUP * NB)
LIFT = 2.0 ** 14
HIGH = lax.Precision.HIGHEST
NT = (((1,), (1,)), ((), ()))
NN = (((1,), (0,)), ((), ()))
F32 = jnp.float32
BF16 = jnp.bfloat16
VMEM = pl.BlockSpec(memory_space=pltpu.VMEM)
HBM = pl.BlockSpec(memory_space=pltpu.HBM)


def dot(a, b, dims=NN, precision=None):
    return lax.dot_general(a, b, dims, precision=precision, preferred_element_type=F32)


def prepare(own_hbm, keys_hbm, q_hbm, out_ref, qx_ref, own_sm, keys_ref, q_ref, sems):
    copies = [
        pltpu.make_async_copy(own_hbm, own_sm, sems.at[0]),
        pltpu.make_async_copy(keys_hbm, keys_ref, sems.at[1]),
        pltpu.make_async_copy(q_hbm, q_ref, sems.at[2]),
    ]
    for copy in copies:
        copy.start()
    for copy in copies:
        copy.wait()
    keys = keys_ref[...]
    blocks = keys.astype(F32)
    kmax = jnp.max(blocks, axis=1)
    kmin = jnp.min(blocks, axis=1)
    kmean = jnp.sum(blocks, axis=1) * (1.0 / BLOCK)
    pos = [jnp.full((1, WIDTH), own_sm[b].astype(F32), F32) for b in range(LOCAL)]
    sub = lax.broadcasted_iota(jnp.int32, (BLOCK, LANES), 0)
    tok = lax.broadcasted_iota(jnp.int32, (BLOCK, LANES), 1) // GROUP
    for b in range(LOCAL):
        s = jnp.where(sub > tok, MASKED, dot(keys[b], q_ref[b], NT))
        ref = jnp.max(s, axis=0, keepdims=True)
        rows = [ref[:, i * WIDTH : (i + 1) * WIDTH] for i in range(LANES // WIDTH)]
        rows += [pos[b], jnp.zeros((11, WIDTH), F32)]
        qx_ref[b, :LANES, :] = q_ref[b]
        qx_ref[b, LANES:, :] = jnp.concatenate(rows, axis=0).astype(BF16)
    pos = jnp.concatenate(pos, axis=0)
    q = q_ref[...].astype(F32).reshape(LOCAL, BLOCK, GROUP, WIDTH)
    qpool = (jnp.sum(q, axis=1) * (1.0 / BLOCK)).reshape(QROWS, WIDTH).astype(BF16)
    extra = jnp.concatenate([kmax, kmin, kmean, pos], axis=0).astype(BF16)
    out_ref[:ROWS, :] = keys.reshape(ROWS, WIDTH)
    out_ref[ROWS:MORE, :] = extra
    out_ref[MORE:, :] = qpool


def maxima(parts):
    row = lax.broadcasted_iota(jnp.int32, parts[0].shape, 0)
    step = 1
    while len(parts) > 1:
        low = (row // step) % 2 == 0
        parts = [
            jnp.maximum(jnp.where(low, a, b), pltpu.roll(jnp.where(low, b, a), 8 - step, 0))
            for a, b in zip(parts[::2], parts[1::2])
        ]
        step *= 2
    return parts[0]


def fold(rows, qb, pb, ref, acc, keep, diag=None):
    for r, row in enumerate(rows):
        for i0 in range(0, HX, 2):
            tiles = [row[i, ROWS:MORE, :].astype(F32)[12:, :] for i in (i0, i0 + 1)]
            pos = jnp.concatenate(tiles, axis=0)
            early, same = pos < pb, pos == pb
            off = jnp.where(early, 0.0, FAR)
            offs = [jnp.broadcast_to(off[j : j + 1, :], (8, WIDTH)) for j in range(8)]
            kept, sums = [], []
            for at in range(0, LANES, 512):
                n = 512 // WIDTH
                base = ref[:, at : at + 512]
                tops = []
                total = acc[:, at : at + 512]
                for i in (0, 1):
                    s = dot(row[i0 + i, :ROWS, :], qb[at : at + 512, :], NT)
                    s = s.reshape(LOCAL, BLOCK // 8, 8, 512)
                    for j in range(LOCAL):
                        tops.append(jnp.max(s[j], axis=0))
                        shift = base + jnp.concatenate([offs[i * LOCAL + j]] * n, axis=1)
                        total = total + jnp.sum(jnp.exp2((s[j] - shift) * EXP2), axis=0)
                sums.append(total)
                top = maxima(tops)
                own = MASKED
                if diag is not None:
                    own = jnp.where(jnp.concatenate([same] * n, axis=1), diag[:, at : at + 512], MASKED)
                kept.append(jnp.where(jnp.concatenate([early] * n, axis=1), top, own))
            acc = jnp.concatenate(sums, axis=1)
            keep(r * HALF, jnp.concatenate(kept, axis=1))
    return acc


def stage(mine, q, mine_ref, q_ref):
    mine_ref[...] = mine[...]
    q_ref[...] = q[...]


def join(mine, beside, out_ref):
    odd = lax.axis_index("x") % 2
    out_ref[odd] = mine[...]
    out_ref[1 - odd] = beside[...]


def start_of(q_ref, b):
    extra = q_ref[b, LANES:, :].astype(F32)
    spread = [jnp.broadcast_to(extra[i : i + 1, :], (8, WIDTH)) for i in range(5)]
    return spread[4], jnp.concatenate(spread[:4], axis=1)


def sweep(*jobs):
    def run(job, b, ref, acc, store):
        rows, q_ref, _, bm_ref, acc_ref, ref_ref, diags = job
        pos, _ = start_of(q_ref, b)
        best = [ref]

        def keep(at, tops):
            best.append(jnp.maximum(best[-1], tops))
            if store:
                bm_ref[b, at : at + 8, :] = tops

        diag = diags[b] if diags is not None else None
        acc_ref[b] = fold(rows, q_ref[b, :LANES, :], pos, ref, acc, keep, diag)
        ref_ref[b] = ref
        return (best[-1] - ref) * EXP2

    worst = jnp.zeros((8, LANES), F32)
    for job in jobs:

        def one(b, worst, job=job):
            return jnp.maximum(worst, run(job, b, *job[2](b), True))

        worst = lax.fori_loop(0, LOCAL, one, worst, unroll=4)

    @pl.when(jnp.max(worst) > 80.0)
    def _():
        for job in jobs:

            def again(b, _, job=job):
                ref, acc = job[2](b)
                high = jnp.maximum(ref, jnp.max(job[3][b], axis=0, keepdims=True))
                run(job, b, high, acc * jnp.exp2((ref - high) * EXP2), False)
                return 0

            lax.fori_loop(0, LOCAL, again, 0)


def held(ref_in, acc_in):
    return lambda b: (ref_in[b], acc_in[b])


def first(q_ref, mine_ref, half, bm_ref, acc_ref, ref_ref, diags):
    sub = lax.broadcasted_iota(jnp.int32, (BLOCK, LANES), 0)
    tok = lax.broadcasted_iota(jnp.int32, (BLOCK, LANES), 1) // GROUP

    def state(b):
        _, ref = start_of(q_ref, b)
        s = jnp.where(sub > tok, MASKED, dot(mine_ref[pl.ds(pl.multiple_of(b * BLOCK, BLOCK), BLOCK), :], q_ref[b, :LANES, :], NT))
        diags[b] = jnp.broadcast_to(jnp.max(s, axis=0, keepdims=True), (8, LANES))
        e = jnp.exp2((s.reshape(BLOCK // 8, 8, LANES) - ref) * EXP2)
        return ref, jnp.sum(e, axis=0)

    sweep(([half], q_ref, state, bm_ref, acc_ref, ref_ref, diags))


def partner_first(q_ref, half, back, ahead, bm_ref, acc_ref, ref_ref):
    def state(b):
        return start_of(q_ref, b)[1], jnp.zeros((8, LANES), F32)

    sweep(([half, back, ahead], q_ref, state, bm_ref, acc_ref, ref_ref, None))


def middle(q_ref, acc_in, ref_in, back, ahead, bm_ref, acc_ref, ref_ref):
    sweep(([back, ahead], q_ref, held(ref_in, acc_in), bm_ref, acc_ref, ref_ref, None))


def both(q0, acc0, ref0, q1, acc1, ref1, back, ahead, bm0, acc0_out, ref0_out, bm1, acc1_out, ref1_out):
    sweep(
        ([back, ahead], q0, held(ref0, acc0), bm0, acc0_out, ref0_out, None),
        ([back, ahead], q1, held(ref1, acc1), bm1, acc1_out, ref1_out, None),
    )


def last_rows(q0, acc0, ref0, q1, acc1, ref1, row, bm0, bm1, stat_ref, a0, r0, a1, r1):
    sweep(
        ([row], q0, held(ref0, acc0), bm0, a0, r0, None),
        ([row], q1, held(ref1, acc1), bm1, a1, r1, None),
    )
    for n, (acc, ref) in enumerate(((a0, r0), (a1, r1))):
        for b in range(LOCAL):
            pair = [jnp.sum(acc[b], axis=0, keepdims=True), ref[b, :1, :]]
            at = (n * LOCAL + b) * 2
            stat_ref[at : at + 2, :] = jnp.concatenate(pair, axis=0)
    extra = row[:, ROWS:, :].astype(F32).reshape(HX * EXTRA, WIDTH)
    wide_rows = [extra[i * CUT : (i + 1) * CUT, :] for i in range(LANES // WIDTH)]
    stat_ref[STATS:, :] = jnp.concatenate(wide_rows, axis=1)


OFFSETS = (0, 7, 1, 6, 2, 5, 3, 4)


def pool(stat, other, *refs):
    bms, (out_ref, tgt) = (refs[:5], refs[5:9]), refs[11:]
    z = lax.axis_index("z")
    lane = lax.broadcasted_iota(jnp.int32, (HALF, WIDTH), 1)
    tgt[...] = jnp.zeros(tgt.shape, F32)
    for n in range(2):
        for b in range(LOCAL):
            here, there = (n * LOCAL + b) * 2, ((1 - n) * LOCAL + b) * 2
            ref0, ref1 = stat[here + 1 : here + 2, :], other[there + 1 : there + 2, :]
            ref = jnp.maximum(ref0, ref1)
            total = stat[here : here + 1, :] * jnp.exp2((ref0 - ref) * EXP2)
            total = total + other[there : there + 1, :] * jnp.exp2((ref1 - ref) * EXP2)
            logsum = jnp.log2(total)
            k = 0
            for bm in bms[n]:
                d = (bm[b] - ref) * EXP2 - logsum
                e = d[:, :WIDTH]
                for i in range(1, LANES // WIDTH):
                    e = jnp.maximum(e, d[:, i * WIDTH : (i + 1) * WIDTH])
                for shift in (8, 16, 32, 64):
                    e = jnp.maximum(e, pltpu.roll(e, shift, 1))
                e = jnp.exp2(e)
                for i in range(bm.shape[1] // HALF):
                    at = pl.multiple_of(lax.rem(z + OFFSETS[k], NZ) * HALF + n * NB // 2, HALF)
                    part = e[i * HALF : (i + 1) * HALF, :]
                    tgt[pl.ds(at, HALF), :] += jnp.where(lane // GROUP == b, part, 0.0)
                    k += 1
    out_ref[...] = tgt[...].T[:QROWS, :] * LIFT


def collect(mine, other, row, stat, qall, kall, posr=None):
    x, z = lax.axis_index("x"), lax.axis_index("z")

    def extra(far, k, i):
        if k < NZ - 1:
            ex = other if far else mine
            return ex[k * HX + i, :16, :].astype(F32), ex[k * HX + i, 16:, :]
        if not far:
            return row[i, ROWS:MORE, :].astype(F32), row[i, MORE:, :]
        low = stat[STATS:, 2 * i * WIDTH : (2 * i + 1) * WIDTH]
        high = stat[STATS:, (2 * i + 1) * WIDTH : (2 * i + 2) * WIDTH]
        return low[:16, :], jnp.concatenate([low[16:, :], high], axis=0).astype(BF16)

    for far, side in ((False, x // 2), (True, 1 - x // 2)):
        for k, off in enumerate(OFFSETS):
            at = lax.rem(z + off, NZ)
            pieces = [extra(far, k, i) for i in range(HX)]
            for part in range(4):
                got = jnp.concatenate([t[4 * part : 4 * part + 4, :] for t, _ in pieces], axis=0)
                to = pl.multiple_of(side * (NB // 2) + at * HALF, HALF)
                kall[part, pl.ds(to, HALF), :] = got
            for i, (tile, queries) in enumerate(pieces):
                to = pl.multiple_of(((side * HX + i) * NZ + at) * QROWS, QROWS)
                qall[pl.ds(to, QROWS), :] = queries
                if posr is not None:
                    rows = [jnp.broadcast_to(tile[12 + b : 13 + b, :], (GROUP, WIDTH)) for b in range(LOCAL)]
                    posr[pl.ds(to, QROWS), :] = jnp.concatenate(rows, axis=0)


def project(kall, wk_ref):
    kproj = jnp.zeros((NB, WIDTH), F32)
    for part in range(3):
        kproj = kproj + dot(kall[part].astype(BF16), wk_ref[part * WIDTH : (part + 1) * WIDTH, :])
    return kproj


def all_targets(got_ref):
    lane = lax.broadcasted_iota(jnp.int32, (NZ * QROWS, WIDTH), 1)
    parts = []
    for x in range(NX):
        own = got_ref[x * NZ : (x + 1) * NZ].reshape(NZ * QROWS, WIDTH)
        far = got_ref[(NX - 1 - x) * NZ : (NX - x) * NZ].reshape(NZ * QROWS, WIDTH)
        row = jnp.where(lane < NB // 2, own, far)
        parts.append(row if x < HX else pltpu.roll(row, NB // 2, 1))
    pooled = jnp.concatenate(parts, axis=0)
    return pooled / jnp.sum(pooled, axis=1, keepdims=True)


def head_loss(got_ref, mine, other, row, stat, wq_ref, wk_ref, out_ref, logp_ref, qall, kall, posr):
    collect(mine, other, row, stat, qall, kall, posr)
    qproj = dot(qall[...], wq_ref[...])
    logits = dot(qproj, project(kall, wk_ref), NT, HIGH) * SCALE
    logits = jnp.where(kall[3].T[:1, :] > posr[...], -1e30, logits)
    shifted = logits - jnp.max(logits, axis=1, keepdims=True)
    logp = shifted - jnp.log(jnp.sum(jnp.exp(shifted), axis=1, keepdims=True))
    logp_ref[...] = logp
    target = all_targets(got_ref)
    safe = jnp.log(jnp.where(target > 0, target, 1.0))
    terms = jnp.where(target > 0, target * (safe - logp), 0.0)
    loss = jnp.sum(jnp.sum(terms, axis=0, keepdims=True), axis=1, keepdims=True) * SHARE
    out_ref[...] = jnp.broadcast_to(loss.reshape(1, 1, 1), out_ref.shape)


def finish(got_ref, logp_ref, mine, other, row, stat, wq_ref, wk_ref, gq_ref, gk_ref, qall, kall):
    collect(mine, other, row, stat, qall, kall)
    target = all_targets(got_ref)
    rowtot = jnp.sum(target, axis=1, keepdims=True)
    dlogit = (jnp.exp(logp_ref[...]) * rowtot - target) * (SHARE * SCALE)
    both = dot(qall[...].astype(F32).T, dlogit, NN, HIGH)
    gq_ref[...] = dot(both, project(kall, wk_ref), NN, HIGH)
    dkproj = dot(wq_ref[...].astype(F32).T, both, NN, HIGH)
    for part in range(3):
        gk_ref[part * WIDTH : (part + 1) * WIDTH, :] = dot(kall[part].T, dkproj, NT, HIGH)


def call(kernel, out_shape, cost, *args, scratch=()):
    return pl.pallas_call(
        kernel,
        out_shape=out_shape,
        in_specs=[VMEM] * len(args),
        out_specs=jax.tree.map(lambda _: VMEM, out_shape),
        scratch_shapes=scratch,
        compiler_params=pltpu.CompilerParams(vmem_limit_bytes=40 << 20),
        cost_estimate=pl.CostEstimate(flops=cost, bytes_accessed=1 << 20, transcendentals=0),
        name=kernel.__name__,
    )(*args)


def shards(queries, keys, block_order, gate_query, gate_key):
    def f32(*shape):
        return jax.ShapeDtypeStruct(shape, F32)

    q4 = queries.reshape(LOCAL, LANES, WIDTH)
    k4 = keys.reshape(LOCAL, BLOCK, WIDTH)
    mine, q0 = pl.pallas_call(
        prepare,
        out_shape=(
            pltpu.VMEM((SENT, WIDTH), BF16),
            pltpu.VMEM((LOCAL, QSENT, WIDTH), BF16),
        ),
        in_specs=[HBM] * 3,
        out_specs=(VMEM, VMEM),
        scratch_shapes=[
            pltpu.SMEM((LOCAL,), jnp.int32),
            pltpu.VMEM(k4.shape, BF16),
            pltpu.VMEM(q4.shape, BF16),
            pltpu.SemaphoreType.DMA((3,)),
        ],
        name="prepare",
    )(block_order, k4, q4)

    def as_one(a):
        return jax.ShapeDtypeStruct(a.shape, a.dtype)

    def partner(a):
        return lax.ppermute(a, "x", [(i, NX - 1 - i) for i in range(NX)])

    def shift(a, by):
        return lax.ppermute(a, "z", [(i, (i + by) % NZ) for i in range(NZ)])

    beside = lax.ppermute(mine, "x", [(i, i ^ 1) for i in range(NX)])
    q1 = partner(q0)
    half = call(join, jax.ShapeDtypeStruct((HX, SENT, WIDTH), BF16), 1 << 10, mine, beside)
    unit = LOCAL * LANES * HALF * BLOCK * WIDTH * 2
    state = (f32(LOCAL, 8, LANES),) * 2

    def maxima_of(n):
        return f32(LOCAL, n * HALF, LANES)

    rows = [half]
    back, ahead = shift(half, 1), shift(half, -1)
    bm, acc, ref = call(
        first, (maxima_of(1),) + state, unit, q0, mine, half,
        scratch=[pltpu.VMEM((LOCAL, 8, LANES), F32)],
    )
    own, other = [bm], []
    for k in range(1, 4):
        back, ahead, acc = lax.optimization_barrier((back, ahead, acc))
        here = (back, ahead)
        rows += here
        back = shift(back, 1)
        ahead = shift(ahead, -1) if k < 3 else None
        if k == 3:
            extras = jnp.concatenate([row[:, ROWS:, :] for row in rows], axis=0)
            far_extras = partner(extras)
        if k == 1:
            bm, acc, ref = call(middle, (maxima_of(2),) + state, 2 * unit, q0, acc, ref, *here)
            q1, acc = lax.optimization_barrier((q1, acc))
            bm1, acc1, ref1 = call(partner_first, (maxima_of(3),) + state, 3 * unit, q1, *rows)
        else:
            bm, acc, ref, bm1, acc1, ref1 = call(
                both, ((maxima_of(2),) + state) * 2, 4 * unit, q0, acc, ref, q1, acc1, ref1, *here
            )
        own.append(bm)
        other.append(bm1)
        acc, acc1 = lax.optimization_barrier((acc, acc1))
    bm0, bm1, stat = call(
        last_rows, (maxima_of(1), maxima_of(1), f32(STATS + CUT, LANES)), 2 * unit,
        q0, acc, ref, q1, acc1, ref1, back,
        scratch=[pltpu.VMEM((LOCAL, 8, LANES), F32)] * 4,
    )
    far_stat, far_extras = lax.optimization_barrier((partner(stat), far_extras))
    pooled = call(
        pool, f32(QROWS, WIDTH), unit // 4, stat, far_stat, *own, bm0, *other, bm1,
        gate_query[0], gate_key[0],
        scratch=[pltpu.VMEM((NB, WIDTH), F32)],
    )
    spread = jnp.broadcast_to(pooled.astype(jnp.float16)[None], (SEQ, QROWS, WIDTH))
    given = (extras, far_extras, back, far_stat, gate_query[0], gate_key[0])
    got = lax.all_to_all(spread, ("x", "z"), 0, 0).astype(F32)
    gathered = [pltpu.VMEM((SEQ * QROWS, WIDTH), BF16), pltpu.VMEM((4, NB, WIDTH), F32)]
    loss, logp = call(
        head_loss, (f32(8, 8, WIDTH), f32(SEQ * QROWS, WIDTH)), unit, got, *given,
        scratch=gathered + [pltpu.VMEM((SEQ * QROWS, WIDTH), F32)],
    )
    loss = lax.all_to_all(loss, ("y", "core"), 0, 0)
    grad_q, grad_k = call(
        finish, (f32(WIDTH, WIDTH), f32(3 * WIDTH, WIDTH)), unit,
        got, logp, *given, scratch=gathered,
    )
    return jnp.sum(loss[:, 0, 0]), grad_q[None], grad_k[None]


def solution(mesh):
    fine = Mesh(mesh.devices.reshape(NX, NZ, 4, 2), ("x", "z", "y", "core"))
    seq, head = ("x", "z"), ("y", "core")
    return jax.shard_map(
        shards,
        mesh=fine,
        in_specs=(
            P(seq, head, None),
            P(seq, head, None),
            P(seq),
            P(head, None, None),
            P(head, None, None),
        ),
        out_specs=(P(), P(head, None, None), P(head, None, None)),
        check_vma=False,
    )
```

```python
import functools
import math

import jax
import jax.numpy as jnp
from jax import lax
from jax.experimental import pallas as pl
from jax.experimental.pallas import tpu as pltpu
from jax.sharding import Mesh, PartitionSpec as P

BLOCK = 64
WIDTH = 128
GROUP = 8
LOCAL = 4
NX, NZ = 4, 8
SEQ = NX * NZ
NB = LOCAL * SEQ
ROWS = LOCAL * BLOCK
MORE = ROWS + 16
SENT = MORE + LOCAL * GROUP
LANES = BLOCK * GROUP
HX = NX // 2
HALF = LOCAL * HX
EXTRA = SENT - ROWS
STATS = 4 * LOCAL
CUT = HX * EXTRA * WIDTH // LANES
QSENT = LANES + 16
QROWS = LOCAL * GROUP
SCALE = WIDTH ** -0.5
EXP2 = SCALE * math.log2(math.e)
MASKED = -1e30 * WIDTH ** 0.5
FAR = 1e30
SHARE = 1.0 / (8 * GROUP * NB)
LIFT = 2.0 ** 14
HIGH = lax.Precision.HIGHEST
NT = (((1,), (1,)), ((), ()))
NN = (((1,), (0,)), ((), ()))
F32 = jnp.float32
BF16 = jnp.bfloat16
VMEM = pl.BlockSpec(memory_space=pltpu.VMEM)
HBM = pl.BlockSpec(memory_space=pltpu.HBM)


def dot(a, b, dims=NN, precision=None):
    return lax.dot_general(a, b, dims, precision=precision, preferred_element_type=F32)


def prepare(own_hbm, keys_hbm, q_hbm, out_ref, qx_ref, own_sm, keys_ref, q_ref, sems):
    copies = [
        pltpu.make_async_copy(own_hbm, own_sm, sems.at[0]),
        pltpu.make_async_copy(keys_hbm, keys_ref, sems.at[1]),
        pltpu.make_async_copy(q_hbm, q_ref, sems.at[2]),
    ]
    for copy in copies:
        copy.start()
    copies[0].wait()
    copies[1].wait()
    keys = keys_ref[...]
    blocks = keys.astype(F32)
    kmax = jnp.max(blocks, axis=1)
    kmin = jnp.min(blocks, axis=1)
    kmean = jnp.sum(blocks, axis=1) * (1.0 / BLOCK)
    pos = [jnp.full((1, WIDTH), own_sm[b].astype(F32), F32) for b in range(LOCAL)]
    sub = lax.broadcasted_iota(jnp.int32, (BLOCK, LANES), 0)
    tok = lax.broadcasted_iota(jnp.int32, (BLOCK, LANES), 1) // GROUP
    copies[2].wait()
    for b in range(LOCAL):
        s = jnp.where(sub > tok, MASKED, dot(keys[b], q_ref[b], NT))
        ref = jnp.max(s, axis=0, keepdims=True)
        ref = ref - jnp.abs(ref) * (1.0 / 128)
        rows = [ref[:, i * WIDTH : (i + 1) * WIDTH] for i in range(LANES // WIDTH)]
        rows += [pos[b], jnp.zeros((11, WIDTH), F32)]
        qx_ref[b, :LANES, :] = q_ref[b]
        qx_ref[b, LANES:, :] = jnp.concatenate(rows, axis=0).astype(BF16)
    pos = jnp.concatenate(pos, axis=0)
    q = q_ref[...].astype(F32).reshape(LOCAL, BLOCK, GROUP, WIDTH)
    qpool = (jnp.sum(q, axis=1) * (1.0 / BLOCK)).reshape(QROWS, WIDTH).astype(BF16)
    extra = jnp.concatenate([kmax, kmin, kmean, pos], axis=0).astype(BF16)
    out_ref[:ROWS, :] = keys.reshape(ROWS, WIDTH)
    out_ref[ROWS:MORE, :] = extra
    out_ref[MORE:, :] = qpool


def maxima(parts):
    row = lax.broadcasted_iota(jnp.int32, parts[0].shape, 0)
    step = 1
    while len(parts) > 1:
        low = (row // step) % 2 == 0
        parts = [
            jnp.maximum(jnp.where(low, a, b), pltpu.roll(jnp.where(low, b, a), 8 - step, 0))
            for a, b in zip(parts[::2], parts[1::2])
        ]
        step *= 2
    return parts[0]


def fold(rows, qb, pb, ref, acc, keep, diag=None):
    for r, row in enumerate(rows):
        for i0 in range(0, HX, 2):
            tiles = [row[i, ROWS:MORE, :].astype(F32)[12:, :] for i in (i0, i0 + 1)]
            pos = jnp.concatenate(tiles, axis=0)
            early, same = pos < pb, pos == pb
            off = jnp.where(early, 0.0, FAR)
            offs = [jnp.broadcast_to(off[j : j + 1, :], (8, WIDTH)) for j in range(8)]
            kept, sums = [], []
            for at in range(0, LANES, 512):
                n = 512 // WIDTH
                base = ref[:, at : at + 512]
                tops = []
                total = acc[:, at : at + 512]
                for i in (0, 1):
                    s = dot(row[i0 + i, :ROWS, :], qb[at : at + 512, :], NT)
                    s = s.reshape(LOCAL, BLOCK // 8, 8, 512)
                    for j in range(LOCAL):
                        tops.append(jnp.max(s[j], axis=0))
                        shift = base + jnp.concatenate([offs[i * LOCAL + j]] * n, axis=1)
                        total = total + jnp.sum(jnp.exp2((s[j] - shift) * EXP2), axis=0)
                sums.append(total)
                top = maxima(tops)
                own = MASKED
                if diag is not None:
                    own = jnp.where(jnp.concatenate([same] * n, axis=1), diag[:, at : at + 512], MASKED)
                kept.append(jnp.where(jnp.concatenate([early] * n, axis=1), top, own))
            acc = jnp.concatenate(sums, axis=1)
            keep(r * HALF, jnp.concatenate(kept, axis=1))
    return acc


def stage(mine, q, mine_ref, q_ref):
    mine_ref[...] = mine[...]
    q_ref[...] = q[...]


def join(mine, beside, out_ref):
    odd = lax.axis_index("x") % 2
    out_ref[odd] = mine[...]
    out_ref[1 - odd] = beside[...]


def start_of(q_ref, b):
    extra = q_ref[b, LANES:, :].astype(F32)
    spread = [jnp.broadcast_to(extra[i : i + 1, :], (8, WIDTH)) for i in range(5)]
    return spread[4], jnp.concatenate(spread[:4], axis=1)


def sweep(*jobs):
    def run(job, b, ref, acc, store):
        rows, q_ref, _, bm_ref, acc_ref, ref_ref, diags = job
        pos, _ = start_of(q_ref, b)
        best = [ref]

        def keep(at, tops):
            best.append(jnp.maximum(best[-1], tops))
            if store:
                bm_ref[b, at : at + 8, :] = tops

        diag = diags[b] if diags is not None else None
        acc_ref[b] = fold(rows, q_ref[b, :LANES, :], pos, ref, acc, keep, diag)
        ref_ref[b] = ref
        return (best[-1] - ref) * EXP2

    worst = jnp.zeros((8, LANES), F32)
    for job in jobs:

        def one(b, worst, job=job):
            return jnp.maximum(worst, run(job, b, *job[2](b), True))

        worst = lax.fori_loop(0, LOCAL, one, worst, unroll=4)

    @pl.when(jnp.max(worst) > 80.0)
    def _():
        for job in jobs:

            def again(b, _, job=job):
                ref, _ = job[2](b)
                high = jnp.maximum(ref, jnp.max(job[3][b], axis=0, keepdims=True))
                run(job, b, *job[2](b, high), False)
                return 0

            lax.fori_loop(0, LOCAL, again, 0)


def held(ref_in, acc_in):
    def state(b, high=None):
        ref, acc = ref_in[b], acc_in[b]
        return (ref, acc) if high is None else (high, acc * jnp.exp2((ref - high) * EXP2))

    return state


def first(q_ref, mine_ref, half, bm_ref, acc_ref, ref_ref, diags):
    sub = lax.broadcasted_iota(jnp.int32, (BLOCK, LANES), 0)
    tok = lax.broadcasted_iota(jnp.int32, (BLOCK, LANES), 1) // GROUP

    def state(b, high=None):
        ref = start_of(q_ref, b)[1] if high is None else high
        s = jnp.where(sub > tok, MASKED, dot(mine_ref[pl.ds(pl.multiple_of(b * BLOCK, BLOCK), BLOCK), :], q_ref[b, :LANES, :], NT))
        diags[b] = jnp.broadcast_to(jnp.max(s, axis=0, keepdims=True), (8, LANES))
        e = jnp.exp2((s.reshape(BLOCK // 8, 8, LANES) - ref) * EXP2)
        return ref, jnp.sum(e, axis=0)

    sweep(([half], q_ref, state, bm_ref, acc_ref, ref_ref, diags))


def partner_first(q_ref, half, back, ahead, bm_ref, acc_ref, ref_ref):
    def state(b, high=None):
        return start_of(q_ref, b)[1] if high is None else high, jnp.zeros((8, LANES), F32)

    sweep(([half, back, ahead], q_ref, state, bm_ref, acc_ref, ref_ref, None))


def middle(q_ref, acc_in, ref_in, back, ahead, bm_ref, acc_ref, ref_ref):
    sweep(([back, ahead], q_ref, held(ref_in, acc_in), bm_ref, acc_ref, ref_ref, None))


def both(q0, acc0, ref0, q1, acc1, ref1, back, ahead, bm0, acc0_out, ref0_out, bm1, acc1_out, ref1_out):
    sweep(
        ([back, ahead], q0, held(ref0, acc0), bm0, acc0_out, ref0_out, None),
        ([back, ahead], q1, held(ref1, acc1), bm1, acc1_out, ref1_out, None),
    )


def last_rows(q0, acc0, ref0, q1, acc1, ref1, row, bm0, bm1, stat_ref, a0, r0, a1, r1):
    sweep(
        ([row], q0, held(ref0, acc0), bm0, a0, r0, None),
        ([row], q1, held(ref1, acc1), bm1, a1, r1, None),
    )
    for n, (acc, ref) in enumerate(((a0, r0), (a1, r1))):
        for b in range(LOCAL):
            pair = [jnp.sum(acc[b], axis=0, keepdims=True), ref[b, :1, :]]
            at = (n * LOCAL + b) * 2
            stat_ref[at : at + 2, :] = jnp.concatenate(pair, axis=0)
    extra = row[:, ROWS:, :].astype(F32).reshape(HX * EXTRA, WIDTH)
    wide_rows = [extra[i * CUT : (i + 1) * CUT, :] for i in range(LANES // WIDTH)]
    stat_ref[STATS:, :] = jnp.concatenate(wide_rows, axis=1)


OFFSETS = (0, 7, 1, 6, 2, 5, 3, 4)


def pool(stat, other, *refs):
    bms, (out_ref, tgt) = (refs[:5], refs[5:9]), refs[11:]
    z = lax.axis_index("z")
    lane = lax.broadcasted_iota(jnp.int32, (HALF, WIDTH), 1)
    tgt[...] = jnp.zeros(tgt.shape, F32)
    for n in range(2):
        for b in range(LOCAL):
            here, there = (n * LOCAL + b) * 2, ((1 - n) * LOCAL + b) * 2
            ref0, ref1 = stat[here + 1 : here + 2, :], other[there + 1 : there + 2, :]
            ref = jnp.maximum(ref0, ref1)
            total = stat[here : here + 1, :] * jnp.exp2((ref0 - ref) * EXP2)
            total = total + other[there : there + 1, :] * jnp.exp2((ref1 - ref) * EXP2)
            logsum = jnp.log2(total)
            k = 0
            for bm in bms[n]:
                d = (bm[b] - ref) * EXP2 - logsum
                e = d[:, :WIDTH]
                for i in range(1, LANES // WIDTH):
                    e = jnp.maximum(e, d[:, i * WIDTH : (i + 1) * WIDTH])
                for shift in (8, 16, 32, 64):
                    e = jnp.maximum(e, pltpu.roll(e, shift, 1))
                e = jnp.exp2(e)
                for i in range(bm.shape[1] // HALF):
                    at = pl.multiple_of(lax.rem(z + OFFSETS[k], NZ) * HALF + n * NB // 2, HALF)
                    part = e[i * HALF : (i + 1) * HALF, :]
                    tgt[pl.ds(at, HALF), :] += jnp.where(lane // GROUP == b, part, 0.0)
                    k += 1
    out_ref[...] = tgt[...].T[:QROWS, :] * LIFT


def collect(mine, other, row, stat, qall, kall, posr=None):
    x, z = lax.axis_index("x"), lax.axis_index("z")

    def extra(far, k, i):
        if k < NZ - 1:
            ex = other if far else mine
            return ex[k * HX + i, :16, :].astype(F32), ex[k * HX + i, 16:, :]
        if not far:
            return row[i, ROWS:MORE, :].astype(F32), row[i, MORE:, :]
        low = stat[STATS:, 2 * i * WIDTH : (2 * i + 1) * WIDTH]
        high = stat[STATS:, (2 * i + 1) * WIDTH : (2 * i + 2) * WIDTH]
        return low[:16, :], jnp.concatenate([low[16:, :], high], axis=0).astype(BF16)

    for far, side in ((False, x // 2), (True, 1 - x // 2)):
        for k, off in enumerate(OFFSETS):
            at = lax.rem(z + off, NZ)
            pieces = [extra(far, k, i) for i in range(HX)]
            for part in range(4):
                got = jnp.concatenate([t[4 * part : 4 * part + 4, :] for t, _ in pieces], axis=0)
                to = pl.multiple_of(side * (NB // 2) + at * HALF, HALF)
                kall[part, pl.ds(to, HALF), :] = got
            for i, (tile, queries) in enumerate(pieces):
                to = pl.multiple_of(((side * HX + i) * NZ + at) * QROWS, QROWS)
                qall[pl.ds(to, QROWS), :] = queries
                if posr is not None:
                    rows = [jnp.broadcast_to(tile[12 + b : 13 + b, :], (GROUP, WIDTH)) for b in range(LOCAL)]
                    posr[pl.ds(to, QROWS), :] = jnp.concatenate(rows, axis=0)


def project(kall, wk_ref):
    kproj = jnp.zeros((NB, WIDTH), F32)
    for part in range(3):
        kproj = kproj + dot(kall[part].astype(BF16), wk_ref[part * WIDTH : (part + 1) * WIDTH, :])
    return kproj


def all_targets(got_ref):
    lane = lax.broadcasted_iota(jnp.int32, (NZ * QROWS, WIDTH), 1)
    parts = []
    for x in range(NX):
        own = got_ref[x * NZ : (x + 1) * NZ].reshape(NZ * QROWS, WIDTH)
        far = got_ref[(NX - 1 - x) * NZ : (NX - x) * NZ].reshape(NZ * QROWS, WIDTH)
        row = jnp.where(lane < NB // 2, own, far)
        parts.append(row if x < HX else pltpu.roll(row, NB // 2, 1))
    pooled = jnp.concatenate(parts, axis=0)
    return pooled / jnp.sum(pooled, axis=1, keepdims=True)


def head_loss(got_ref, mine, other, row, stat, wq_ref, wk_ref, out_ref, logp_ref, qall, kall, posr):
    collect(mine, other, row, stat, qall, kall, posr)
    qproj = dot(qall[...], wq_ref[...])
    logits = dot(qproj, project(kall, wk_ref), NT, HIGH) * SCALE
    logits = jnp.where(kall[3].T[:1, :] > posr[...], -1e30, logits)
    shifted = logits - jnp.max(logits, axis=1, keepdims=True)
    logp = shifted - jnp.log(jnp.sum(jnp.exp(shifted), axis=1, keepdims=True))
    logp_ref[...] = logp
    target = all_targets(got_ref)
    safe = jnp.log(jnp.where(target > 0, target, 1.0))
    terms = jnp.where(target > 0, target * (safe - logp), 0.0)
    loss = jnp.sum(jnp.sum(terms, axis=0, keepdims=True), axis=1, keepdims=True) * SHARE
    out_ref[...] = jnp.broadcast_to(loss.reshape(1, 1, 1), out_ref.shape)


def finish(got_ref, logp_ref, mine, other, row, stat, wq_ref, wk_ref, gq_ref, gk_ref, qall, kall):
    collect(mine, other, row, stat, qall, kall)
    target = all_targets(got_ref)
    rowtot = jnp.sum(target, axis=1, keepdims=True)
    dlogit = (jnp.exp(logp_ref[...]) * rowtot - target) * (SHARE * SCALE)
    both = dot(qall[...].astype(F32).T, dlogit, NN, HIGH)
    gq_ref[...] = dot(both, project(kall, wk_ref), NN, HIGH)
    dkproj = dot(wq_ref[...].astype(F32).T, both, NN, HIGH)
    for part in range(3):
        gk_ref[part * WIDTH : (part + 1) * WIDTH, :] = dot(kall[part].T, dkproj, NT, HIGH)


def call(kernel, out_shape, cost, *args, scratch=()):
    return pl.pallas_call(
        kernel,
        out_shape=out_shape,
        in_specs=[VMEM] * len(args),
        out_specs=jax.tree.map(lambda _: VMEM, out_shape),
        scratch_shapes=scratch,
        compiler_params=pltpu.CompilerParams(vmem_limit_bytes=40 << 20),
        cost_estimate=pl.CostEstimate(flops=cost, bytes_accessed=1 << 20, transcendentals=0),
        name=kernel.__name__,
    )(*args)


def shards(queries, keys, block_order, gate_query, gate_key):
    def f32(*shape):
        return jax.ShapeDtypeStruct(shape, F32)

    q4 = queries.reshape(LOCAL, LANES, WIDTH)
    k4 = keys.reshape(LOCAL, BLOCK, WIDTH)
    mine, q0 = pl.pallas_call(
        prepare,
        out_shape=(
            pltpu.VMEM((SENT, WIDTH), BF16),
            pltpu.VMEM((LOCAL, QSENT, WIDTH), BF16),
        ),
        in_specs=[HBM] * 3,
        out_specs=(VMEM, VMEM),
        scratch_shapes=[
            pltpu.SMEM((LOCAL,), jnp.int32),
            pltpu.VMEM(k4.shape, BF16),
            pltpu.VMEM(q4.shape, BF16),
            pltpu.SemaphoreType.DMA((3,)),
        ],
        name="prepare",
    )(block_order, k4, q4)

    def as_one(a):
        return jax.ShapeDtypeStruct(a.shape, a.dtype)

    def partner(a):
        return lax.ppermute(a, "x", [(i, NX - 1 - i) for i in range(NX)])

    def shift(a, by):
        return lax.ppermute(a, "z", [(i, (i + by) % NZ) for i in range(NZ)])

    beside = lax.ppermute(mine, "x", [(i, i ^ 1) for i in range(NX)])
    q1 = partner(q0)
    half = call(join, jax.ShapeDtypeStruct((HX, SENT, WIDTH), BF16), 1 << 10, mine, beside)
    unit = LOCAL * LANES * HALF * BLOCK * WIDTH * 2
    state = (f32(LOCAL, 8, LANES),) * 2

    def maxima_of(n):
        return f32(LOCAL, n * HALF, LANES)

    rows = [half]
    back, ahead = shift(half, 1), shift(half, -1)
    bm, acc, ref = call(
        first, (maxima_of(1),) + state, unit, q0, mine, half,
        scratch=[pltpu.VMEM((LOCAL, 8, LANES), F32)],
    )
    own, other = [bm], []
    for k in range(1, 4):
        back, ahead, acc = lax.optimization_barrier((back, ahead, acc))
        here = (back, ahead)
        rows += here
        back = shift(back, 1)
        ahead = shift(ahead, -1) if k < 3 else None
        if k == 3:
            extras = jnp.concatenate([row[:, ROWS:, :] for row in rows], axis=0)
            far_extras = partner(extras)
        if k == 1:
            bm, acc, ref = call(middle, (maxima_of(2),) + state, 2 * unit, q0, acc, ref, *here)
            q1, acc = lax.optimization_barrier((q1, acc))
            bm1, acc1, ref1 = call(partner_first, (maxima_of(3),) + state, 3 * unit, q1, *rows)
        else:
            bm, acc, ref, bm1, acc1, ref1 = call(
                both, ((maxima_of(2),) + state) * 2, 4 * unit, q0, acc, ref, q1, acc1, ref1, *here
            )
        own.append(bm)
        other.append(bm1)
        acc, acc1 = lax.optimization_barrier((acc, acc1))
    bm0, bm1, stat = call(
        last_rows, (maxima_of(1), maxima_of(1), f32(STATS + CUT, LANES)), 2 * unit,
        q0, acc, ref, q1, acc1, ref1, back,
        scratch=[pltpu.VMEM((LOCAL, 8, LANES), F32)] * 4,
    )
    far_stat, far_extras = lax.optimization_barrier((partner(stat), far_extras))
    pooled = call(
        pool, f32(QROWS, WIDTH), unit // 4, stat, far_stat, *own, bm0, *other, bm1,
        gate_query[0], gate_key[0],
        scratch=[pltpu.VMEM((NB, WIDTH), F32)],
    )
    spread = jnp.broadcast_to(pooled.astype(jnp.float16)[None], (SEQ, QROWS, WIDTH))
    given = (extras, far_extras, back, far_stat, gate_query[0], gate_key[0])
    got = lax.all_to_all(spread, ("x", "z"), 0, 0).astype(F32)
    gathered = [pltpu.VMEM((SEQ * QROWS, WIDTH), BF16), pltpu.VMEM((4, NB, WIDTH), F32)]
    loss, logp = call(
        head_loss, (f32(8, 8, WIDTH), f32(SEQ * QROWS, WIDTH)), unit, got, *given,
        scratch=gathered + [pltpu.VMEM((SEQ * QROWS, WIDTH), F32)],
    )
    loss = lax.all_to_all(loss, ("y", "core"), 0, 0)
    grad_q, grad_k = call(
        finish, (f32(WIDTH, WIDTH), f32(3 * WIDTH, WIDTH)), unit,
        got, logp, *given, scratch=gathered,
    )
    return jnp.sum(loss[:, 0, 0]), grad_q[None], grad_k[None]


def solution(mesh):
    fine = Mesh(mesh.devices.reshape(NX, NZ, 4, 2), ("x", "z", "y", "core"))
    seq, head = ("x", "z"), ("y", "core")
    return jax.shard_map(
        shards,
        mesh=fine,
        in_specs=(
            P(seq, head, None),
            P(seq, head, None),
            P(seq),
            P(head, None, None),
            P(head, None, None),
        ),
        out_specs=(P(), P(head, None, None), P(head, None, None)),
        check_vma=False,
    )
```
